512 devices in a mesh: ctx: 64 (over y, z), tp: 8 (over x, core).
Axes of the slice: x: 4, y: 4, z: 16, core: 2. Of those that a mesh axis runs over, the one named last changes fastest.
Arguments:
- query_rows: bfloat16 [8192, 4096], P('ctx', 'tp'), may hold values from -6 to 6
- key_rows: bfloat16 [8192, 4096], P('ctx', 'tp'), may hold values from -0.5 to 0.5
- value_rows: bfloat16 [8192, 4096], P('ctx', 'tp'), may hold values from -40 to 40
- position: int32 [8192], P('ctx'), may hold values from 0 to 8191, as said below
- lengths: int32 [32], replicated, may hold values from 1 to 512, 8192 in all
- decay_rates: float32 [32], P('tp'), may hold values from 0.0001953125 to 0.0333333333
- norm_gain: float32 [4096], P('tp'), may hold values from 0.5 to 1.5
- grad_output: bfloat16 [8192, 4096], P('ctx', 'tp'), may hold values from -6 to 6
Outputs:
- normed: bfloat16 [8192, 4096], P('ctx', 'tp')
- grad_query: bfloat16 [8192, 4096], P('ctx', 'tp')
- grad_key: bfloat16 [8192, 4096], P('ctx', 'tp')
- grad_value: bfloat16 [8192, 4096], P('ctx', 'tp')
The draws below stay inside these ranges and needn't reach their ends.
Inputs may be any that keep to these rules, and one draw needn't show every extreme that they name: position is a permutation of the 8192 places; among the rows of one device at most 4 lie in one block of 128 places, and in every draw every device has a block with exactly 4. lengths sum to 8192; the longest is exactly 512.
All inputs are finite; a program needn't handle non-finite values.
Results may differ from the reference program's by a relative error of at most 0.012.
Values may be sent and summed in bfloat16 or wider, within the bound.
A program may use at most 128 MiB of HBM per device.

```python
import math
import jax
import jax.numpy as jnp
import numpy as np
from jax import lax

HEADS = 32
HD = 128
ROWS = 128
SPAN = 4
TOKENS = 8192
MOST = 512
DOCS = 32


def draw_position(key, part):
    key = jax.random.fold_in(key, 11)
    loaders = TOKENS // ROWS
    quota_rows = ROWS // loaders
    half_count = loaders // 2
    keys_all = jax.random.split(key, 5)
    swing = jax.random.randint(keys_all[0], (half_count,), -quota_rows, quota_rows + 1)
    swing = swing.at[0].set(quota_rows)
    weights = jnp.concatenate([quota_rows + swing, quota_rows - swing]).astype(jnp.int32)
    row_perm = jax.random.permutation(keys_all[1], loaders)
    col_perm = jax.random.permutation(keys_all[2], loaders)
    counts = weights[(row_perm[:, None] + col_perm[None, :]) % loaders]
    row_ends = jnp.cumsum(counts, axis=1)
    row_start = row_ends - counts
    col_start = jnp.cumsum(counts, axis=0) - counts
    slot_ids = jnp.arange(ROWS, dtype=jnp.int32)
    owners = jnp.sum((row_ends[:, None, :] <= slot_ids[None, :, None]).astype(jnp.int32), axis=2)
    rank_in = slot_ids[None, :] - jnp.take_along_axis(row_start, owners, axis=1)
    within = jnp.take_along_axis(col_start, owners, axis=1) + rank_in
    owner_perm = jax.vmap(lambda sub_key: jax.random.permutation(sub_key, ROWS))(jax.random.split(keys_all[3], loaders))
    placed = owners * ROWS + owner_perm[owners, within]
    loader_perm = jax.vmap(lambda sub_key: jax.random.permutation(sub_key, ROWS))(jax.random.split(keys_all[4], loaders))
    final = jnp.take_along_axis(placed, loader_perm, axis=1)
    return final.reshape(TOKENS).astype(jnp.int32)


def draw_decay_rates(key, part):
    key = jax.random.fold_in(key, 23)
    keys_all = jax.random.split(key, 3)
    chooser = jax.random.uniform(keys_all[0], (HEADS,), jnp.float32)
    share = 0.5
    fast_rate = jnp.exp(jax.random.uniform(keys_all[1], (HEADS,), jnp.float32, jnp.log(1.0 / 50.0), jnp.log(1.0 / 30.0)))
    slow_rate = jnp.exp(jax.random.uniform(keys_all[2], (HEADS,), jnp.float32, jnp.log(0.1), 0.0)) / (SPAN * ROWS)
    return jnp.where(chooser < share, slow_rate, fast_rate).astype(jnp.float32)


def draw_value_rows(key, part):
    key = jax.random.fold_in(key, 37)
    keys_all = jax.random.split(key, 2)
    head_of = jnp.arange(HEADS * HD) // HD
    jitter = jnp.clip(jax.random.normal(keys_all[1], (HEADS,), jnp.float32), -2.0, 2.0)
    level = jnp.exp(jnp.log(3.0) * head_of.astype(jnp.float32) / (HEADS - 1) + 0.3 * jitter[head_of])
    base = jnp.clip(jax.random.normal(keys_all[0], (TOKENS, HEADS * HD), jnp.float32), -4.0, 4.0)
    return (base * level[None, :]).astype(jnp.bfloat16)


def levels(own_key, dims, cuts, low, high):
    loudness, own = 1.0, jax.random.fold_in(own_key, 6)
    for dim, parts in cuts:
        steps = jnp.exp(jax.random.uniform(jax.random.fold_in(own, dim), (parts,), jnp.float32, low / len(cuts), high / len(cuts)))
        loudness = loudness * jnp.repeat(steps, dims[dim] // parts).reshape([-1 if axis == dim else 1 for axis in range(len(dims))])
    return loudness


def length_profile(count, total, most, lean):
    weights = [(1 << 20) // math.isqrt(standing ** lean) + 1 for standing in range(2, count + 1)]
    rest, given = total - most - (count - 1), [1] * (count - 1)
    while rest > 0:
        candidates = [i for i in range(count - 1) if given[i] < most]
        mass, remaining = sum([weights[i] for i in candidates]), rest
        for i in candidates:
            extra = min(most - given[i], max(1, remaining * weights[i] // mass), rest)
            given[i] = given[i] + extra
            rest = rest - extra
    return np.array([most] + given)


def ragged(own_key, count, total, reach, lean):
    if count == 2:
        one = jax.random.randint(own_key, (), max(1, total - reach), min(reach, total - 1) + 1)
        return jnp.stack([one, total - one])
    sizes = jnp.asarray(length_profile(count, total, reach, lean), jnp.int32)
    couples = (count - 1) // 2
    source_of, taker = sizes[1:1 + 2 * couples:2], sizes[2:2 + 2 * couples:2]
    slack = jnp.minimum(source_of - 1, reach - taker)
    shifted = jax.random.randint(jax.random.fold_in(own_key, 1), (couples,), 0, 1 << 20) % (slack + 1)
    sizes = sizes.at[1:1 + 2 * couples:2].set(source_of - shifted).at[2:2 + 2 * couples:2].set(taker + shifted)
    return sizes[jax.random.permutation(jax.random.fold_in(own_key, 2), count)]


def normal_values(rng, shape, scale, limit, pieces=(), held_as=jnp.bfloat16):
    array = jax.random.normal(rng, shape, jnp.float32) * scale
    if len(pieces) > 0:
        array = levels(rng, shape, pieces, -0.22, 0.18) * array
    return jnp.clip(array, min=-limit, max=limit).astype(held_as)


def setup_inputs(seed: int = 0) -> dict:
    seeds = jax.random.split(jax.random.key(seed), 9)
    return {
        "query_rows": normal_values(seeds[0], (TOKENS, HEADS * HD), 1.0, 6.0, ((0, 64), (1, 8))),
        "key_rows": normal_values(seeds[1], (TOKENS, HEADS * HD), HD ** -0.5, 0.5, ((0, 64), (1, 8))),
        "value_rows": draw_value_rows(jax.random.fold_in(seeds[8], 71), 0),
        "position": draw_position(jax.random.fold_in(seeds[8], 71), 0),
        "lengths": ragged(seeds[4], DOCS, TOKENS, MOST, 2).astype(jnp.int32),
        "decay_rates": draw_decay_rates(jax.random.fold_in(seeds[8], 71), 0),
        "norm_gain": jnp.clip(1.0 + 0.1 * jax.random.normal(seeds[6], (HEADS * HD,), jnp.float32), 0.5, 1.5),
        "grad_output": normal_values(seeds[7], (TOKENS, HEADS * HD), 1.0, 6.0, ((0, 64), (1, 8))),
    }


epsilon = 1e-05
highest = lax.Precision.HIGHEST

def doc_index(doc_starts, places):
    return lax.optimization_barrier(jnp.sum((doc_starts[None, :] <= places[:, None]).astype(jnp.int32), axis=1)) - 1

def block_masks(doc_ids, doc_prev, doc_next, decay_rates, row_pos, block_rows):
    row_gap = row_pos[:, None] - row_pos[None, :]
    causal = row_gap >= 0.0
    decay_grid = jnp.exp(-decay_rates[:, None, None] * jnp.maximum(row_gap, 0.0)[None, :, :])
    same_doc = (doc_ids[:, None] == doc_ids[None, :]) & causal
    weight = jnp.where(same_doc[None, :, :], decay_grid, 0.0)
    enter_weight = jnp.where((doc_ids == doc_prev)[:, None], jnp.exp(-decay_rates[None, :] * (row_pos[:, None] + 1.0)), 0.0)
    leave_weight = jnp.where((doc_ids == doc_next)[:, None], jnp.exp(-decay_rates[None, :] * (block_rows - row_pos[:, None])), 0.0)
    own_end = jnp.where((doc_ids == doc_ids[-1])[:, None], jnp.exp(-decay_rates[None, :] * (block_rows - 1.0 - row_pos[:, None])), 0.0)
    own_start = jnp.where((doc_ids == doc_ids[0])[:, None], jnp.exp(-decay_rates[None, :] * row_pos[:, None]), 0.0)
    span_decay = jnp.exp(-decay_rates * block_rows)
    fwd_factor = jnp.where(doc_prev == doc_ids[-1], span_decay, 0.0)
    bwd_factor = jnp.where(doc_ids[0] == doc_next, span_decay, 0.0)
    return (weight, enter_weight, leave_weight, own_end, own_start, fwd_factor, bwd_factor)

def reference(query_rows, key_rows, value_rows, position, lengths, decay_rates, norm_gain, grad_output):
    tokens, feat_width = query_rows.shape
    head_count = decay_rates.shape[0]
    head_dim = feat_width // head_count
    blocks = tokens // ROWS
    stacked = jnp.concatenate([query_rows, key_rows, value_rows], axis=1)
    packed = jnp.zeros((tokens, 3 * feat_width), stacked.dtype).at[position].set(stacked)
    shape_four = (blocks, ROWS, head_count, head_dim)
    query_all = packed[:, :feat_width].reshape(shape_four)
    key_all = packed[:, feat_width:2 * feat_width].reshape(shape_four)
    value_all = packed[:, 2 * feat_width:].reshape(shape_four)
    doc_starts = jnp.cumsum(lengths) - lengths
    doc_all = doc_index(doc_starts, jnp.arange(tokens, dtype=jnp.int32)).reshape(blocks, ROWS)
    block_starts = jnp.arange(blocks, dtype=jnp.int32) * ROWS
    doc_prev_all = doc_index(doc_starts, block_starts - 1)
    after_ids = doc_index(doc_starts, jnp.minimum(block_starts + ROWS, tokens - 1))
    doc_next_all = jnp.where(block_starts + ROWS < tokens, after_ids, -2)
    row_pos = jnp.arange(ROWS, dtype=jnp.float32)

    def forward(state_in, inputs):
        query_block, key_block, value_block, doc_ids, doc_prev, doc_next = inputs
        weight, enter_weight, leave_weight, own_end, own_start, fwd_factor, bwd_factor = block_masks(doc_ids, doc_prev, doc_next, decay_rates, row_pos, ROWS)
        query_f = query_block.astype(jnp.float32)
        key_f = key_block.astype(jnp.float32)
        value_f = value_block.astype(jnp.float32)
        scores = jnp.einsum('phd,shd->hps', query_f, key_f)
        probs_bf = lax.optimization_barrier((scores * weight).astype(jnp.bfloat16))
        intra_term = jnp.einsum('hps,shd->phd', probs_bf.astype(jnp.float32), value_f)
        inter_term = jnp.einsum('phd,hde->phe', query_f * enter_weight[:, :, None], state_in, precision=highest)
        attention = (intra_term + inter_term).astype(jnp.bfloat16)
        local_state = jnp.einsum('shd,she->hde', key_f * own_end[:, :, None], value_f, precision=highest)
        state_out = fwd_factor[:, None, None] * state_in + local_state
        return (state_out, (attention, state_in))
    zero_state = jnp.zeros((head_count, head_dim, head_dim), jnp.float32)
    unused, (attention_all, entered_all) = lax.scan(forward, zero_state, (query_all, key_all, value_all, doc_all, doc_prev_all, doc_next_all))
    attention_bf = lax.optimization_barrier(attention_all.reshape(tokens, feat_width))
    attn_f = attention_bf.astype(jnp.float32)
    inverse = lax.rsqrt(lax.optimization_barrier(jnp.mean(attn_f * attn_f, axis=1)) + epsilon)
    normed = (attn_f * inverse[:, None] * norm_gain).astype(jnp.bfloat16)
    grad_f = grad_output.astype(jnp.float32) * norm_gain
    cross_sum = lax.optimization_barrier(jnp.sum(grad_f * attn_f, axis=1))
    grad_attn = (inverse[:, None] * grad_f - attn_f * (inverse ** 3 * cross_sum / feat_width)[:, None]).astype(jnp.bfloat16)
    grad_attn = lax.optimization_barrier(grad_attn).reshape(shape_four)

    def backward(state_out, inputs):
        query_block, key_block, value_block, grad_block, doc_ids, doc_prev, doc_next, entered = inputs
        weight, enter_weight, leave_weight, own_end, own_start, fwd_factor, bwd_factor = block_masks(doc_ids, doc_prev, doc_next, decay_rates, row_pos, ROWS)
        query_f = query_block.astype(jnp.float32)
        key_f = key_block.astype(jnp.float32)
        value_f = value_block.astype(jnp.float32)
        grad_blk_f = grad_block.astype(jnp.float32)
        scores = jnp.einsum('phd,shd->hps', query_f, key_f)
        probs_bf = lax.optimization_barrier((scores * weight).astype(jnp.bfloat16))
        grad_scores = jnp.einsum('phd,shd->hps', grad_blk_f, value_f)
        grad_probs = lax.optimization_barrier((grad_scores * weight).astype(jnp.bfloat16))
        probs_f = probs_bf.astype(jnp.float32)
        gprobs_f = grad_probs.astype(jnp.float32)
        grad_q = jnp.einsum('hps,shd->phd', gprobs_f, key_f) + jnp.einsum('phe,hde->phd', grad_blk_f * enter_weight[:, :, None], entered, precision=highest)
        grad_k = jnp.einsum('hps,phd->shd', gprobs_f, query_f) + jnp.einsum('she,hde->shd', value_f * leave_weight[:, :, None], state_out, precision=highest)
        grad_v = jnp.einsum('hps,phd->shd', probs_f, grad_blk_f) + jnp.einsum('shd,hde->she', key_f * leave_weight[:, :, None], state_out, precision=highest)
        local_back = jnp.einsum('phd,phe->hde', query_f * own_start[:, :, None], grad_blk_f, precision=highest)
        state_back = bwd_factor[:, None, None] * state_out + local_back
        return (state_back, (grad_q.astype(jnp.bfloat16), grad_k.astype(jnp.bfloat16), grad_v.astype(jnp.bfloat16)))
    unused_back, (grad_q_all, grad_k_all, grad_v_all) = lax.scan(backward, zero_state, (query_all, key_all, value_all, grad_attn, doc_all, doc_prev_all, doc_next_all, entered_all), reverse=True)
    grad_packed = jnp.concatenate([grad_q_all.reshape(tokens, feat_width), grad_k_all.reshape(tokens, feat_width), grad_v_all.reshape(tokens, feat_width)], axis=1)
    grad_loaded = grad_packed[position]
    return (normed, grad_loaded[:, :feat_width], grad_loaded[:, feat_width:2 * feat_width], grad_loaded[:, 2 * feat_width:])
```

```python
import jax
import jax.numpy as jnp
from jax import lax
from jax.experimental import pallas as pl
from jax.experimental.pallas import tpu as pltpu
from jax.sharding import PartitionSpec as P

MESH = pl.DeviceIdType.MESH
F32, BF16, I32 = jnp.float32, jnp.bfloat16, jnp.int32
HIGHEST = lax.Precision.HIGHEST
EPSILON = 1e-05
ROWS = 128
HD = 128
JOIN = 4
SPAN = JOIN * ROWS
CTX, TP = 64, 8
GROUPS = CTX // JOIN
CAP = 4 * JOIN
SLOTS = GROUPS * CAP
ARRIVE = CTX * CAP
WIDE = 3 * HD


def dot(a, b, precision=None):
    return jnp.dot(a, b, preferred_element_type=F32, precision=precision)


def dot_nt(a, b, precision=None):
    return lax.dot_general(a, b, (((1,), (1,)), ((), ())), preferred_element_type=F32, precision=precision)


def dot_tn(a, b):
    return lax.dot_general(a, b, (((0,), (0,)), ((), ())), preferred_element_type=F32)


def iota(shape, dim):
    return lax.broadcasted_iota(I32, shape, dim)


def onehot(condition):
    return jnp.where(condition, 1.0, 0.0).astype(BF16)


def column(row):
    return jnp.broadcast_to(row, (ROWS, ROWS)).T


def kernel(
    pos_ref, len_ref, rate_ref, gain_ref, q_ref, k_ref, v_ref, go_ref,
    nrm_ref, dq_ref, dk_ref, dv_ref,
    snd, rcv, snd2, rcv2, pls, plr, u_ref, ut_ref, w_ref, ends, qx, kx, vx, gox, att, dob, pb, dpb,
    nsend, state, state_in, back, back_in, part, ar1, sub, ar2, ssem, rsem,
):
    c, t = lax.axis_index("ctx"), lax.axis_index("tp")
    grp, k = c // JOIN, lax.rem(c, JOIN)
    own_cols = pl.ds(pl.multiple_of(k * HD, HD), HD)

    barrier = pltpu.get_barrier_semaphore()

    @pl.loop(1, CTX)
    def _(d):
        pl.semaphore_signal(barrier, inc=1, device_id={"ctx": lax.rem(c + d, CTX)}, device_id_type=MESH)

    @pl.loop(1, TP)
    def _(d):
        pl.semaphore_signal(barrier, inc=1, device_id={"tp": lax.rem(t + d, TP)}, device_id_type=MESH)

    def remote(src, dst, index, **where):
        return pltpu.make_async_remote_copy(
            src_ref=src, dst_ref=dst, send_sem=ssem.at[index], recv_sem=rsem.at[index],
            device_id=where, device_id_type=MESH,
        )

    def wait(ref, sems, index):
        pltpu.make_async_copy(ref, ref, sems.at[index]).wait()

    def peer(d):
        f = CTX - d
        turn, dy = f // 4, lax.rem(f, 4)
        h = (turn + 1) // 2
        dz = jnp.where(lax.rem(turn, 2) == 1, h, 16 - h)
        return lax.rem(c // 16 + dy, 4) * 16 + lax.rem(lax.rem(c, 16) + dz, 16)

    pos = pos_ref[...]
    posr = jnp.broadcast_to(pos, (ROWS, ROWS))
    posc = posr.T
    gr, gc = posr >> 9, posc >> 9
    ri, ci = iota((ROWS, ROWS), 0), iota((ROWS, ROWS), 1)
    same = gr == gc
    rank_row = jnp.sum(jnp.where(same & (ri < ci), 1, 0), axis=0, keepdims=True)
    rank_col = jnp.sum(jnp.where(same & (ci < ri), 1, 0), axis=1, keepdims=True)
    slot_row = gr[:1] * CAP + rank_row
    slot_col = gc[:, :1] * CAP + rank_col
    place = (pos & (SPAN - 1)) + 1
    holds = jnp.where(iota((GROUPS, ROWS), 0) == gr[:1], place, 0).astype(F32)
    ranked = jnp.where(ci == rank_col, 1.0, 0.0)
    pls[...] = dot(holds, ranked, HIGHEST) - 1.0
    pick = onehot(iota((SLOTS, ROWS), 0) == slot_row)

    def spread(ref, part_index):
        moved = dot(pick, ref[...]).astype(BF16)
        for h in range(JOIN):
            snd[:, h, :, part_index * HD : (part_index + 1) * HD] = moved[:, h * HD : (h + 1) * HD].reshape(
                GROUPS, CAP, HD
            )

    spread(k_ref, 0)
    spread(v_ref, 1)
    spread(q_ref, 2)
    pl.semaphore_wait(barrier, CTX - 1 + TP - 1)

    @pl.loop(1, CTX)
    def _(d):
        p = peer(d)
        remote(pls.at[pl.ds(p // JOIN, 1)], plr.at[pl.ds(c, 1)], 0, ctx=p).start()
        remote(
            snd.at[p // JOIN, lax.rem(p, JOIN), :, pl.ds(0, 2 * HD)],
            rcv.at[pl.ds(c * CAP, CAP), pl.ds(0, 2 * HD)],
            1, ctx=p,
        ).start()

    def mates(fn):
        for d in range(1, JOIN):
            m = lax.rem(k + d, JOIN)
            fn(m, grp * JOIN + m)

    mates(
        lambda m, p: remote(
            go_ref.at[:, pl.ds(pl.multiple_of(m * HD, HD), HD)], gox.at[pl.ds(k * ROWS, ROWS)], 3, ctx=p
        ).start()
    )

    @pl.loop(1, CTX)
    def _(d):
        p = peer(d)
        remote(
            snd.at[p // JOIN, lax.rem(p, JOIN), :, pl.ds(2 * HD, HD)],
            rcv.at[pl.ds(c * CAP, CAP), pl.ds(2 * HD, HD)],
            2, ctx=p,
        ).start()

    rcv[pl.ds(c * CAP, CAP)] = snd[grp, k]
    plr[pl.ds(c, 1)] = pls[pl.ds(grp, 1)]
    gox[pl.ds(k * ROWS, ROWS)] = go_ref[:, own_cols]

    rate = rate_ref[k]
    start = grp * SPAN
    here = iota((1, SPAN), 1) + start
    doc_row = jnp.full((1, SPAN), -1, I32)
    offset = jnp.int32(0)
    doc_prev, doc_next = jnp.int32(-1), jnp.int32(-1)
    doc_first, doc_last = jnp.int32(-1), jnp.int32(-1)
    for d in range(len_ref.shape[0]):
        doc_row += jnp.where(offset <= here, 1, 0)
        doc_prev += jnp.where(offset <= start - 1, 1, 0)
        doc_first += jnp.where(offset <= start, 1, 0)
        doc_last += jnp.where(offset <= start + SPAN - 1, 1, 0)
        doc_next += jnp.where(offset <= start + SPAN, 1, 0)
        offset += len_ref[d]
    doc_next = jnp.where(grp == GROUPS - 1, -2, doc_next)
    for i in range(JOIN):
        rows = slice(i * ROWS, (i + 1) * ROWS)
        doc_col = column(doc_row[:, rows])
        for j in range(i + 1):
            gap = (ri - ci) + (i - j) * ROWS
            kept = doc_col == doc_row[:, j * ROWS : (j + 1) * ROWS]
            if i == j:
                kept = kept & (gap >= 0)
            decay = jnp.exp(-rate * jnp.maximum(gap, 0).astype(F32))
            w_ref[rows, j * ROWS : (j + 1) * ROWS] = jnp.where(kept, decay, 0.0)
        at = (ri + i * ROWS).astype(F32)
        ends[0, rows] = jnp.where(doc_col == doc_prev, jnp.exp(-rate * (at + 1.0)), 0.0)
        ends[1, rows] = jnp.where(doc_col == doc_next, jnp.exp(-rate * (SPAN - at)), 0.0)
        ends[2, rows] = jnp.where(doc_col == doc_last, jnp.exp(-rate * (SPAN - 1.0 - at)), 0.0)
        ends[3, rows] = jnp.where(doc_col == doc_first, jnp.exp(-rate * at), 0.0)

    wait(plr.at[pl.ds(0, CTX - 1)], rsem, 0)
    places = plr[...]
    tile = jnp.where(lax.rem(iota((ROWS, ARRIVE), 1), CAP) == iota((ROWS, ARRIVE), 0), 1.0, 0.0)
    owner = iota((CTX, ARRIVE), 1) // CAP == iota((CTX, ARRIVE), 0)
    place_row = jnp.sum(jnp.where(owner, dot(places, tile, HIGHEST), 0.0), axis=0, keepdims=True)
    place_row = place_row.astype(I32)
    for i in range(JOIN):
        rows = slice(i * ROWS, (i + 1) * ROWS)
        u_ref[rows] = onehot(iota((ROWS, ARRIVE), 0) + i * ROWS == place_row)
    for j in range(ARRIVE // ROWS):
        cols = slice(j * ROWS, (j + 1) * ROWS)
        place_col = column(place_row[:, cols])
        for i in range(JOIN):
            ut_ref[cols, i * ROWS : (i + 1) * ROWS] = onehot(place_col == ci + i * ROWS)

    wait(rcv.at[pl.ds(0, ARRIVE - CAP), pl.ds(0, 2 * HD)], rsem, 1)
    kv = dot(u_ref[...], rcv[:, : 2 * HD]).astype(BF16)
    kx[...] = kv[:, :HD]
    vx[...] = kv[:, HD:]
    state[...] = dot_tn((kx[...].astype(F32) * ends[2]).astype(BF16), vx[...]).astype(BF16)
    remote(state, state_in, 4, ctx=lax.rem(c + JOIN, CTX)).start()

    wait(rcv.at[pl.ds(0, ARRIVE - CAP), pl.ds(2 * HD, HD)], rsem, 2)
    qx[...] = dot(u_ref[...], rcv[:, 2 * HD :]).astype(BF16)
    for i in range(JOIN):
        rows, n = slice(i * ROWS, (i + 1) * ROWS), (i + 1) * ROWS
        pb[rows, :n] = (dot_nt(qx[rows], kx[:n]) * w_ref[rows, :n]).astype(BF16)
    wait(gox.at[pl.ds(0, SPAN - ROWS)], rsem, 3)
    wait(state_in, rsem, 4)
    gain = gain_ref[:, own_cols]
    ones = jnp.ones((8, HD), F32)
    for i in range(JOIN):
        rows, n = slice(i * ROWS, (i + 1) * ROWS), (i + 1) * ROWS
        entered = (qx[rows].astype(F32) * ends[0, rows]).astype(BF16)
        a = (dot(pb[rows, :n], vx[:n]) + dot(entered, state_in[...])).astype(BF16)
        att[rows] = a
        a = a.astype(F32)
        g = gox[rows].astype(F32) * gain
        part[:, i * ROWS : (i + 1) * ROWS] = dot_nt(ones, a * a, HIGHEST)[:1]
        part[:, SPAN + i * ROWS : SPAN + (i + 1) * ROWS] = dot_nt(ones, g * a, HIGHEST)[:1]

    mates(lambda m, p: remote(part, ar1.at[k], 5, ctx=p).start())
    ar1[k] = part[...]
    wait(ar1.at[pl.ds(0, JOIN - 1)], rsem, 5)
    sub[...] = ar1[0] + ar1[1] + ar1[2] + ar1[3]
    for d in range(1, TP):
        remote(sub, ar2.at[t], 6, tp=lax.rem(t + d, TP)).start()
    ar2[t] = sub[...]
    wait(ar2.at[pl.ds(0, TP - 1)], rsem, 6)
    total = ar2[0]
    for d in range(1, TP):
        total += ar2[d]
    width = float(HD * JOIN * TP)
    inverse = lax.rsqrt(total[:, :SPAN] / width + EPSILON)
    coef = inverse * inverse * inverse * total[:, SPAN:] / width

    carried = jnp.zeros((HD, HD), F32)
    for i in range(JOIN):
        rows = slice(i * ROWS, (i + 1) * ROWS)
        inv, cf = column(inverse[:, rows]), column(coef[:, rows])
        a = att[rows].astype(F32)
        g = gox[rows].astype(F32) * gain
        d_o = (inv * g - a * cf).astype(BF16)
        dob[rows] = d_o
        nsend[i] = (a * inv * gain).astype(BF16)
        carried += dot_tn((qx[rows].astype(F32) * ends[3, rows]).astype(BF16), d_o)
    back[...] = carried.astype(BF16)
    remote(back, back_in, 8, ctx=lax.rem(c + CTX - JOIN, CTX)).start()

    def send_back(lo, n, index):
        @pl.loop(1, CTX)
        def _(d):
            p = peer(d)
            remote(
                snd2.at[pl.ds(p * CAP, CAP), pl.ds(lo, n)],
                rcv2.at[k, pl.ds(grp * CAP, CAP), pl.ds(lo, n)],
                index, ctx=p,
            ).start()

    dq = []
    for i in range(JOIN):
        rows, n = slice(i * ROWS, (i + 1) * ROWS), (i + 1) * ROWS
        dp = (dot_nt(dob[rows], vx[:n]) * w_ref[rows, :n]).astype(BF16)
        dpb[rows, :n] = dp
        entered = (dob[rows].astype(F32) * ends[0, rows]).astype(BF16)
        dq.append((dot(dp, kx[:n]) + dot_nt(entered, state_in[...])).astype(BF16))
    snd2[:, :HD] = dot(ut_ref[...], jnp.concatenate(dq, axis=0)).astype(BF16)
    send_back(0, HD, 9)
    mates(lambda m, p: remote(nsend.at[m], nrm_ref.at[:, own_cols], 7, ctx=p).start())
    nrm_ref[:, own_cols] = nsend[k]

    wait(back_in, rsem, 8)
    dk, dv = [], []
    for j in range(JOIN):
        cols, low = slice(j * ROWS, (j + 1) * ROWS), j * ROWS
        leave = ends[1, cols]
        value = (vx[cols].astype(F32) * leave).astype(BF16)
        key = (kx[cols].astype(F32) * leave).astype(BF16)
        dk.append((dot_tn(dpb[low:, cols], qx[low:]) + dot_nt(value, back_in[...])).astype(BF16))
        dv.append((dot_tn(pb[low:, cols], dob[low:]) + dot(key, back_in[...])).astype(BF16))
    both = jnp.concatenate([jnp.concatenate(dk, axis=0), jnp.concatenate(dv, axis=0)], axis=1)
    snd2[:, HD:] = dot(ut_ref[...], both).astype(BF16)
    send_back(HD, 2 * HD, 10)
    rcv2[k, pl.ds(grp * CAP, CAP)] = snd2[pl.ds(c * CAP, CAP)]

    give = onehot(iota((ROWS, SLOTS), 1) == slot_col)
    wait(snd2.at[pl.ds(0, ARRIVE - CAP), pl.ds(0, HD)], rsem, 9)
    for h in range(JOIN):
        dq_ref[:, h * HD : (h + 1) * HD] = dot(give, rcv2[h, :, :HD]).astype(BF16)
    wait(snd2.at[pl.ds(0, ARRIVE - CAP), pl.ds(HD, 2 * HD)], rsem, 10)
    for h in range(JOIN):
        moved = dot(give, rcv2[h, :, HD:]).astype(BF16)
        dk_ref[:, h * HD : (h + 1) * HD] = moved[:, :HD]
        dv_ref[:, h * HD : (h + 1) * HD] = moved[:, HD:]
    wait(nsend.at[pl.ds(0, JOIN - 1)], rsem, 7)

    wait(plr.at[pl.ds(0, CTX - 1)], ssem, 0)
    wait(rcv.at[pl.ds(0, ARRIVE - CAP), pl.ds(0, 2 * HD)], ssem, 1)
    wait(rcv.at[pl.ds(0, ARRIVE - CAP), pl.ds(2 * HD, HD)], ssem, 2)
    wait(gox.at[pl.ds(0, SPAN - ROWS)], ssem, 3)
    wait(state, ssem, 4)
    wait(ar1.at[pl.ds(0, JOIN - 1)], ssem, 5)
    wait(ar2.at[pl.ds(0, TP - 1)], ssem, 6)
    wait(nsend.at[pl.ds(0, JOIN - 1)], ssem, 7)
    wait(back, ssem, 8)
    wait(snd2.at[pl.ds(0, ARRIVE - CAP), pl.ds(0, HD)], ssem, 9)
    wait(snd2.at[pl.ds(0, ARRIVE - CAP), pl.ds(HD, 2 * HD)], ssem, 10)


def body(query_rows, key_rows, value_rows, position, lengths, decay_rates, norm_gain, grad_output):
    vmem, smem = pl.BlockSpec(memory_space=pltpu.VMEM), pl.BlockSpec(memory_space=pltpu.SMEM)
    shape = jax.ShapeDtypeStruct(query_rows.shape, BF16)
    return pl.pallas_call(
        kernel,
        out_shape=(shape,) * 4,
        in_specs=[vmem, smem, smem] + [vmem] * 5,
        out_specs=(vmem,) * 4,
        scratch_shapes=[
            pltpu.VMEM((GROUPS, JOIN, CAP, WIDE), BF16),
            pltpu.VMEM((ARRIVE, WIDE), BF16),
            pltpu.VMEM((ARRIVE, WIDE), BF16),
            pltpu.VMEM((JOIN, SLOTS, WIDE), BF16),
            pltpu.VMEM((GROUPS, ROWS), F32),
            pltpu.VMEM((CTX, ROWS), F32),
            pltpu.VMEM((SPAN, ARRIVE), BF16),
            pltpu.VMEM((ARRIVE, SPAN), BF16),
            pltpu.VMEM((SPAN, SPAN), F32),
            pltpu.VMEM((4, SPAN, HD), F32),
            pltpu.VMEM((SPAN, HD), BF16),
            pltpu.VMEM((SPAN, HD), BF16),
            pltpu.VMEM((SPAN, HD), BF16),
            pltpu.VMEM((SPAN, HD), BF16),
            pltpu.VMEM((SPAN, HD), BF16),
            pltpu.VMEM((SPAN, HD), BF16),
            pltpu.VMEM((SPAN, SPAN), BF16),
            pltpu.VMEM((SPAN, SPAN), BF16),
            pltpu.VMEM((JOIN, ROWS, HD), BF16),
            pltpu.VMEM((HD, HD), BF16),
            pltpu.VMEM((HD, HD), BF16),
            pltpu.VMEM((HD, HD), BF16),
            pltpu.VMEM((HD, HD), BF16),
            pltpu.VMEM((1, 2 * SPAN), F32),
            pltpu.VMEM((JOIN, 1, 2 * SPAN), F32),
            pltpu.VMEM((1, 2 * SPAN), F32),
            pltpu.VMEM((TP, 1, 2 * SPAN), F32),
            pltpu.SemaphoreType.DMA((11,)),
            pltpu.SemaphoreType.DMA((11,)),
        ],
        compiler_params=pltpu.CompilerParams(
            collective_id=0, has_side_effects=True, vmem_limit_bytes=40 << 20
        ),
        name="lightning",
    )(
        position.reshape(1, ROWS), lengths, decay_rates, norm_gain.reshape(1, -1),
        query_rows, key_rows, value_rows, grad_output,
    )


def solution(mesh):
    rows, specs = P("ctx", "tp"), (P("ctx", "tp"),) * 4
    return jax.shard_map(
        body,
        mesh=mesh,
        in_specs=(rows, rows, rows, P("ctx"), P(), P("tp"), P("tp"), rows),
        out_specs=specs,
        check_vma=False,
    )
```

```python
import jax
import jax.numpy as jnp
from jax import lax
from jax.experimental import pallas as pl
from jax.experimental.pallas import tpu as pltpu
from jax.sharding import PartitionSpec as P

MESH = pl.DeviceIdType.MESH
F32, BF16, I32 = jnp.float32, jnp.bfloat16, jnp.int32
HIGHEST = lax.Precision.HIGHEST
EPSILON = 1e-05
ROWS = 128
HD = 128
JOIN = 4
SPAN = JOIN * ROWS
CTX, TP = 64, 8
GROUPS = CTX // JOIN
CAP = 4 * JOIN
SLOTS = GROUPS * CAP
ARRIVE = CTX * CAP
WIDE = 3 * HD


def dot(a, b, precision=None):
    return jnp.dot(a, b, preferred_element_type=F32, precision=precision)


def dot_nt(a, b, precision=None):
    return lax.dot_general(a, b, (((1,), (1,)), ((), ())), preferred_element_type=F32, precision=precision)


def dot_tn(a, b):
    return lax.dot_general(a, b, (((0,), (0,)), ((), ())), preferred_element_type=F32)


def iota(shape, dim):
    return lax.broadcasted_iota(I32, shape, dim)


def onehot(condition):
    return jnp.where(condition, 1.0, 0.0).astype(BF16)


def column(row):
    return jnp.broadcast_to(row, (ROWS, ROWS)).T


def kernel(
    pos_hbm, len_hbm, rate_hbm, gain_hbm, q_hbm, k_hbm, v_hbm, go_hbm,
    nrm_out, dq_out, got, give_out,
    pos_ref, len_ref, rate_ref, gain_ref, q_ref, k_ref, v_ref, go_ref, lsem,
    snd, rcv, sndq, snd2, pall, u_ref, ut_ref, w_ref, ends, qx, kx, vx, gox, att, attx, dob, pb, dpb,
    nrm_ref, dq_ref, give_ref, rcvq, state, state_in, back, back_in, part, ar1, sub, ar2, inv_ref, ssem, rsem,
):
    c, t = lax.axis_index("ctx"), lax.axis_index("tp")
    grp, k = c // JOIN, lax.rem(c, JOIN)
    own_cols = pl.ds(pl.multiple_of(k * HD, HD), HD)

    loads = [
        pltpu.make_async_copy(src, dst, lsem.at[i])
        for i, (src, dst) in enumerate(
            (
                (pos_hbm, pos_ref), (k_hbm, k_ref), (v_hbm, v_ref), (q_hbm, q_ref),
                (len_hbm, len_ref), (rate_hbm, rate_ref), (gain_hbm, gain_ref), (go_hbm, go_ref),
            )
        )
    ]
    for load in loads:
        load.start()
    barrier = pltpu.get_barrier_semaphore()

    @pl.loop(1, CTX)
    def _(d):
        pl.semaphore_signal(barrier, inc=1, device_id={"ctx": lax.rem(c + d, CTX)}, device_id_type=MESH)

    @pl.loop(1, TP)
    def _(d):
        pl.semaphore_signal(barrier, inc=1, device_id={"tp": lax.rem(t + d, TP)}, device_id_type=MESH)

    def remote(src, dst, index, **where):
        return pltpu.make_async_remote_copy(
            src_ref=src, dst_ref=dst, send_sem=ssem.at[index], recv_sem=rsem.at[index],
            device_id=where, device_id_type=MESH,
        )

    def wait(ref, sems, index):
        pltpu.make_async_copy(ref, ref, sems.at[index]).wait()

    def peer(d):
        f = CTX - d
        turn, dy = f // 4, lax.rem(f, 4)
        h = (turn + 1) // 2
        dz = jnp.where(lax.rem(turn, 2) == 1, h, 16 - h)
        return lax.rem(c // 16 + dy, 4) * 16 + lax.rem(lax.rem(c, 16) + dz, 16)

    loads[0].wait()
    pos = pos_ref[...]
    posr = jnp.broadcast_to(pos, (ROWS, ROWS))
    posc = posr.T
    gr, gc = posr >> 9, posc >> 9
    ri, ci = iota((ROWS, ROWS), 0), iota((ROWS, ROWS), 1)
    same = gr == gc
    rank_row = jnp.sum(jnp.where(same & (ri < ci), 1, 0), axis=0, keepdims=True)
    rank_col = jnp.sum(jnp.where(same & (ci < ri), 1, 0), axis=1, keepdims=True)
    slot_row = gr[:1] * CAP + rank_row
    slot_col = gc[:, :1] * CAP + rank_col
    pick = onehot(iota((SLOTS, ROWS), 0) == slot_row)

    def spread(ref, part_index):
        moved = dot(pick, ref[...]).astype(BF16)
        for h in range(JOIN):
            snd[:, h, :, part_index * HD : (part_index + 1) * HD] = moved[:, h * HD : (h + 1) * HD].reshape(
                GROUPS, CAP, HD
            )

    for i, ref in enumerate((k_ref, v_ref, q_ref)):
        loads[i + 1].wait()
        spread(ref, i)
    pl.semaphore_wait(barrier, CTX - 1 + TP - 1)

    own_y, own_z = c // 16, lax.rem(c, 16)

    @pl.loop(1, 16)
    def _(d):
        remote(pos_ref, pall.at[pl.ds(c, 1)], 0, ctx=own_y * 16 + lax.rem(own_z + d, 16)).start()

    def send_rows(lo, n, index):
        @pl.loop(1, CTX)
        def _(d):
            p = peer(d)
            remote(
                snd.at[p // JOIN, lax.rem(p, JOIN), :, pl.ds(lo, n)],
                rcv.at[pl.ds(c * CAP, CAP), pl.ds(lo, n)],
                index, ctx=p,
            ).start()

    send_rows(0, 2 * HD, 1)
    send_rows(2 * HD, HD, 2)

    def mates(fn):
        for d in range(1, JOIN):
            m = lax.rem(k + d, JOIN)
            fn(m, grp * JOIN + m)

    rcv[pl.ds(c * CAP, CAP)] = snd[grp, k]
    pall[pl.ds(c, 1)] = pos
    give_ref[...] = onehot(iota((ROWS, SLOTS), 1) == slot_col)
    stores = [pltpu.make_async_copy(give_ref, give_out, lsem.at[8])]
    stores[0].start()
    for load in loads[4:]:
        load.wait()
    gox[pl.ds(k * ROWS, ROWS)] = go_ref[:, own_cols]

    rate = rate_ref[k]
    start = grp * SPAN
    here = iota((1, SPAN), 1) + start
    doc_row = jnp.full((1, SPAN), -1, I32)
    offset = jnp.int32(0)
    doc_prev, doc_next = jnp.int32(-1), jnp.int32(-1)
    doc_first, doc_last = jnp.int32(-1), jnp.int32(-1)
    for d in range(len_ref.shape[0]):
        doc_row += jnp.where(offset <= here, 1, 0)
        doc_prev += jnp.where(offset <= start - 1, 1, 0)
        doc_first += jnp.where(offset <= start, 1, 0)
        doc_last += jnp.where(offset <= start + SPAN - 1, 1, 0)
        doc_next += jnp.where(offset <= start + SPAN, 1, 0)
        offset += len_ref[d]
    doc_next = jnp.where(grp == GROUPS - 1, -2, doc_next)
    for i in range(JOIN):
        rows = slice(i * ROWS, (i + 1) * ROWS)
        doc_col = column(doc_row[:, rows])
        for j in range(i + 1):
            gap = (ri - ci) + (i - j) * ROWS
            kept = doc_col == doc_row[:, j * ROWS : (j + 1) * ROWS]
            if i == j:
                kept = kept & (gap >= 0)
            decay = jnp.exp(-rate * jnp.maximum(gap, 0).astype(F32))
            w_ref[rows, j * ROWS : (j + 1) * ROWS] = jnp.where(kept, decay, 0.0)
        at = (ri + i * ROWS).astype(F32)
        ends[0, rows] = jnp.where(doc_col == doc_prev, jnp.exp(-rate * (at + 1.0)), 0.0)
        ends[1, rows] = jnp.where(doc_col == doc_next, jnp.exp(-rate * (SPAN - at)), 0.0)
        ends[2, rows] = jnp.where(doc_col == doc_last, jnp.exp(-rate * (SPAN - 1.0 - at)), 0.0)
        ends[3, rows] = jnp.where(doc_col == doc_first, jnp.exp(-rate * at), 0.0)

    wait(pall.at[pl.ds(0, 15)], rsem, 0)
    own_line = pall.at[pl.ds(pl.multiple_of(own_y * 16, 16), 16)]
    for d in range(1, 4):
        remote(own_line, own_line, 9, ctx=lax.rem(own_y + d, 4) * 16 + own_z).start()
    wait(pall.at[pl.ds(0, 48)], rsem, 9)
    everywhere = pall[...]
    ours = everywhere >> 9 == grp
    rank = dot(onehot(ours), onehot(ri < ci))
    place = (everywhere & (SPAN - 1)).astype(F32) + 1.0
    places = jnp.zeros((CTX, ROWS), F32)
    for r in range(CAP):
        held = jnp.sum(jnp.where(ours & (rank == float(r)), place, 0.0), axis=1, keepdims=True)
        places = jnp.where(iota((CTX, ROWS), 1) == r, held, places)
    tile = jnp.where(lax.rem(iota((ROWS, ARRIVE), 1), CAP) == iota((ROWS, ARRIVE), 0), 1.0, 0.0)
    owner = iota((CTX, ARRIVE), 1) // CAP == iota((CTX, ARRIVE), 0)
    place_row = jnp.sum(jnp.where(owner, dot(places, tile, HIGHEST), 0.0), axis=0, keepdims=True) - 1.0
    place_row = place_row.astype(I32)
    for i in range(JOIN):
        rows = slice(i * ROWS, (i + 1) * ROWS)
        u_ref[rows] = onehot(iota((ROWS, ARRIVE), 0) + i * ROWS == place_row)
    for j in range(ARRIVE // ROWS):
        cols = slice(j * ROWS, (j + 1) * ROWS)
        place_col = column(place_row[:, cols])
        for i in range(JOIN):
            ut_ref[cols, i * ROWS : (i + 1) * ROWS] = onehot(place_col == ci + i * ROWS)

    wait(rcv.at[pl.ds(0, ARRIVE - CAP), pl.ds(0, 2 * HD)], rsem, 1)
    kv = dot(u_ref[...], rcv[:, : 2 * HD]).astype(BF16)
    kx[...] = kv[:, :HD]
    vx[...] = kv[:, HD:]
    state[...] = dot_tn((kx[...].astype(F32) * ends[2]).astype(BF16), vx[...]).astype(BF16)
    remote(state, state_in, 4, ctx=lax.rem(c + JOIN, CTX)).start()

    wait(rcv.at[pl.ds(0, ARRIVE - CAP), pl.ds(2 * HD, HD)], rsem, 2)
    mates(
        lambda m, p: remote(
            go_ref.at[:, pl.ds(pl.multiple_of(m * HD, HD), HD)], gox.at[pl.ds(k * ROWS, ROWS)], 3, ctx=p
        ).start()
    )
    qx[...] = dot(u_ref[...], rcv[:, 2 * HD :]).astype(BF16)
    for i in range(JOIN):
        rows, n = slice(i * ROWS, (i + 1) * ROWS), (i + 1) * ROWS
        pb[rows, :n] = (dot_nt(qx[rows], kx[:n]) * w_ref[rows, :n]).astype(BF16)
    wait(state_in, rsem, 4)
    gain = gain_ref[:, own_cols]
    ones = jnp.ones((8, HD), BF16)

    def row_sums(x):
        high = x.astype(BF16)
        low = (x - high.astype(F32)).astype(BF16)
        return (dot_nt(ones, high) + dot_nt(ones, low))[:1]

    for i in range(JOIN):
        rows, n = slice(i * ROWS, (i + 1) * ROWS), (i + 1) * ROWS
        entered = (qx[rows].astype(F32) * ends[0, rows]).astype(BF16)
        a = (dot(pb[rows, :n], vx[:n]) + dot(entered, state_in[...])).astype(BF16)
        att[rows] = a
        a = a.astype(F32)
        part[:, i * ROWS : (i + 1) * ROWS] = row_sums(a * a)
    wait(gox.at[pl.ds(0, SPAN - ROWS)], rsem, 3)
    for i in range(JOIN):
        rows = slice(i * ROWS, (i + 1) * ROWS)
        g = gox[rows].astype(F32) * gain
        part[:, SPAN + i * ROWS : SPAN + (i + 1) * ROWS] = row_sums(g * att[rows].astype(F32))

    for d in range(1, TP):
        remote(part, ar2.at[t], 6, tp=lax.rem(t + d, TP)).start()
    mates(
        lambda m, p: remote(
            att.at[pl.ds(pl.multiple_of(m * ROWS, ROWS), ROWS)], attx.at[:, own_cols], 7, ctx=p
        ).start()
    )
    attx[:, own_cols] = att[pl.ds(pl.multiple_of(k * ROWS, ROWS), ROWS)]
    ar2[t] = part[...]
    wait(ar2.at[pl.ds(0, TP - 1)], rsem, 6)
    total = ar2[0]
    for d in range(1, TP):
        total += ar2[d]
    sub[...] = total
    mates(lambda m, p: remote(sub, ar1.at[k], 5, ctx=p).start())
    ar1[k] = total
    wait(ar1.at[pl.ds(0, JOIN - 1)], rsem, 5)
    total = ar1[0] + ar1[1] + ar1[2] + ar1[3]
    width = float(HD * JOIN * TP)
    inverse = lax.rsqrt(total[:, :SPAN] / width + EPSILON)
    coef = inverse * inverse * inverse * total[:, SPAN:] / width
    inv_ref[...] = inverse

    carried = jnp.zeros((HD, HD), F32)
    for i in range(JOIN):
        rows = slice(i * ROWS, (i + 1) * ROWS)
        inv, cf = column(inverse[:, rows]), column(coef[:, rows])
        a = att[rows].astype(F32)
        g = gox[rows].astype(F32) * gain
        d_o = (inv * g - a * cf).astype(BF16)
        dob[rows] = d_o
        carried += dot_tn((qx[rows].astype(F32) * ends[3, rows]).astype(BF16), d_o)
    back[...] = carried.astype(BF16)
    remote(back, back_in, 8, ctx=lax.rem(c + CTX - JOIN, CTX)).start()

    def send_back(src, dst, index):
        @pl.loop(1, CTX)
        def _(d):
            p = peer(d)
            remote(src.at[pl.ds(p * CAP, CAP)], dst.at[k, pl.ds(grp * CAP, CAP)], index, ctx=p).start()

    dq = []
    for i in range(JOIN):
        rows, n = slice(i * ROWS, (i + 1) * ROWS), (i + 1) * ROWS
        dp = (dot_nt(dob[rows], vx[:n]) * w_ref[rows, :n]).astype(BF16)
        dpb[rows, :n] = dp
        entered = (dob[rows].astype(F32) * ends[0, rows]).astype(BF16)
        dq.append((dot(dp, kx[:n]) + dot_nt(entered, state_in[...])).astype(BF16))
    sndq[...] = dot(ut_ref[...], jnp.concatenate(dq, axis=0)).astype(BF16)
    send_back(sndq, rcvq, 10)
    rcvq[k, pl.ds(grp * CAP, CAP)] = sndq[pl.ds(c * CAP, CAP)]

    wait(back_in, rsem, 8)
    dk, dv = [], []
    for j in range(JOIN):
        cols, low = slice(j * ROWS, (j + 1) * ROWS), j * ROWS
        leave = ends[1, cols]
        value = (vx[cols].astype(F32) * leave).astype(BF16)
        key = (kx[cols].astype(F32) * leave).astype(BF16)
        dk.append((dot_tn(dpb[low:, cols], qx[low:]) + dot_nt(value, back_in[...])).astype(BF16))
        dv.append((dot_tn(pb[low:, cols], dob[low:]) + dot(key, back_in[...])).astype(BF16))
    both = jnp.concatenate([jnp.concatenate(dk, axis=0), jnp.concatenate(dv, axis=0)], axis=1)
    snd2[...] = dot(ut_ref[...], both).astype(BF16)
    send_back(snd2, got, 11)
    stores.append(
        pltpu.make_async_copy(snd2.at[pl.ds(c * CAP, CAP)], got.at[k, pl.ds(grp * CAP, CAP)], lsem.at[9])
    )
    stores[-1].start()

    wait(att.at[pl.ds(0, SPAN - ROWS)], rsem, 7)
    inv = column(inv_ref[:, own_cols])
    for h in range(JOIN):
        cols = slice(h * HD, (h + 1) * HD)
        nrm_ref[:, cols] = (attx[:, cols].astype(F32) * inv * gain_ref[:, cols]).astype(BF16)
    stores.append(pltpu.make_async_copy(nrm_ref, nrm_out, lsem.at[10]))
    stores[-1].start()

    wait(sndq.at[pl.ds(0, ARRIVE - CAP)], rsem, 10)
    for h in range(JOIN):
        dq_ref[:, h * HD : (h + 1) * HD] = dot(give_ref[...], rcvq[h]).astype(BF16)
    stores.append(pltpu.make_async_copy(dq_ref, dq_out, lsem.at[11]))
    stores[-1].start()
    wait(snd2.at[pl.ds(0, ARRIVE - CAP)], rsem, 11)

    wait(pall.at[pl.ds(0, 15)], ssem, 0)
    wait(rcv.at[pl.ds(0, ARRIVE - CAP), pl.ds(0, 2 * HD)], ssem, 1)
    wait(rcv.at[pl.ds(0, ARRIVE - CAP), pl.ds(2 * HD, HD)], ssem, 2)
    wait(gox.at[pl.ds(0, SPAN - ROWS)], ssem, 3)
    wait(state, ssem, 4)
    wait(ar1.at[pl.ds(0, JOIN - 1)], ssem, 5)
    wait(ar2.at[pl.ds(0, TP - 1)], ssem, 6)
    wait(att.at[pl.ds(0, SPAN - ROWS)], ssem, 7)
    wait(back, ssem, 8)
    wait(pall.at[pl.ds(0, 48)], ssem, 9)
    wait(sndq.at[pl.ds(0, ARRIVE - CAP)], ssem, 10)
    wait(snd2.at[pl.ds(0, ARRIVE - CAP)], ssem, 11)
    for store in stores:
        store.wait()


def finish(nrm, dq, got, give, nrm_out, dq_out, dk_out, dv_out, *scratch):
    nrm_ref, dq_ref, got_ref, give_ref, dk_ref, dv_ref, sem = scratch
    loads = [
        pltpu.make_async_copy(src, dst, sem.at[i])
        for i, (src, dst) in enumerate(((give, give_ref), (got, got_ref), (nrm, nrm_ref), (dq, dq_ref)))
    ]
    stores = [
        pltpu.make_async_copy(src, dst, sem.at[4 + i])
        for i, (src, dst) in enumerate(((dk_ref, dk_out), (dv_ref, dv_out), (nrm_ref, nrm_out), (dq_ref, dq_out)))
    ]
    for load in loads:
        load.start()
    for load in loads[:2]:
        load.wait()
    for i, ref in enumerate((dk_ref, dv_ref)):
        for h in range(JOIN):
            moved = dot(give_ref[...], got_ref[h, :, i * HD : (i + 1) * HD])
            ref[:, h * HD : (h + 1) * HD] = moved.astype(BF16)
        stores[i].start()
    for load, store in zip(loads[2:], stores[2:]):
        load.wait()
        store.start()
    for store in stores:
        store.wait()


def body(query_rows, key_rows, value_rows, position, lengths, decay_rates, norm_gain, grad_output):
    hbm = pl.BlockSpec(memory_space=pltpu.HBM)
    shape = jax.ShapeDtypeStruct(query_rows.shape, BF16)
    held = pltpu.VMEM(query_rows.shape, BF16)
    kept = pl.pallas_call(
        kernel,
        out_shape=(
            shape, shape,
            jax.ShapeDtypeStruct((JOIN, SLOTS, 2 * HD), BF16), jax.ShapeDtypeStruct((ROWS, SLOTS), BF16),
        ),
        in_specs=[hbm] * 8,
        out_specs=(hbm,) * 4,
        scratch_shapes=[
            pltpu.VMEM((1, ROWS), I32),
            pltpu.SMEM(lengths.shape, I32),
            pltpu.SMEM(decay_rates.shape, F32),
            pltpu.VMEM((1, JOIN * HD), F32),
            held, held, held, held,
            pltpu.SemaphoreType.DMA((12,)),
            pltpu.VMEM((GROUPS, JOIN, CAP, WIDE), BF16),
            pltpu.VMEM((ARRIVE, WIDE), BF16),
            pltpu.VMEM((ARRIVE, HD), BF16),
            pltpu.VMEM((ARRIVE, 2 * HD), BF16),
            pltpu.VMEM((CTX, ROWS), I32),
            pltpu.VMEM((SPAN, ARRIVE), BF16),
            pltpu.VMEM((ARRIVE, SPAN), BF16),
            pltpu.VMEM((SPAN, SPAN), F32),
            pltpu.VMEM((4, SPAN, HD), F32),
            pltpu.VMEM((SPAN, HD), BF16),
            pltpu.VMEM((SPAN, HD), BF16),
            pltpu.VMEM((SPAN, HD), BF16),
            pltpu.VMEM((SPAN, HD), BF16),
            pltpu.VMEM((SPAN, HD), BF16),
            held,
            pltpu.VMEM((SPAN, HD), BF16),
            pltpu.VMEM((SPAN, SPAN), BF16),
            pltpu.VMEM((SPAN, SPAN), BF16),
            held, held,
            pltpu.VMEM((ROWS, SLOTS), BF16),
            pltpu.VMEM((JOIN, SLOTS, HD), BF16),
            pltpu.VMEM((HD, HD), BF16),
            pltpu.VMEM((HD, HD), BF16),
            pltpu.VMEM((HD, HD), BF16),
            pltpu.VMEM((HD, HD), BF16),
            pltpu.VMEM((1, 2 * SPAN), F32),
            pltpu.VMEM((JOIN, 1, 2 * SPAN), F32),
            pltpu.VMEM((1, 2 * SPAN), F32),
            pltpu.VMEM((TP, 1, 2 * SPAN), F32),
            pltpu.VMEM((1, SPAN), F32),
            pltpu.SemaphoreType.DMA((12,)),
            pltpu.SemaphoreType.DMA((12,)),
        ],
        compiler_params=pltpu.CompilerParams(
            collective_id=0, has_side_effects=True, vmem_limit_bytes=60 << 20
        ),
        name="lightning",
    )(
        position.reshape(1, ROWS), lengths, decay_rates, norm_gain.reshape(1, -1),
        query_rows, key_rows, value_rows, grad_output,
    )
    return pl.pallas_call(
        finish,
        out_shape=(shape,) * 4,
        in_specs=[hbm] * 4,
        out_specs=(hbm,) * 4,
        scratch_shapes=[
            held, held, pltpu.VMEM((JOIN, SLOTS, 2 * HD), BF16), pltpu.VMEM((ROWS, SLOTS), BF16),
            held, held, pltpu.SemaphoreType.DMA((8,)),
        ],
        compiler_params=pltpu.CompilerParams(vmem_limit_bytes=60 << 20),
        name="finish",
    )(*kept)


def solution(mesh):
    rows, specs = P("ctx", "tp"), (P("ctx", "tp"),) * 4
    return jax.shard_map(
        body,
        mesh=mesh,
        in_specs=(rows, rows, rows, P("ctx"), P(), P("tp"), P("tp"), rows),
        out_specs=specs,
        check_vma=False,
    )
```

```python
import jax
import jax.numpy as jnp
from jax import lax
from jax.experimental import pallas as pl
from jax.experimental.pallas import tpu as pltpu
from jax.sharding import PartitionSpec as P

MESH = pl.DeviceIdType.MESH
F32, BF16, I32 = jnp.float32, jnp.bfloat16, jnp.int32
HIGHEST = lax.Precision.HIGHEST
EPSILON = 1e-05
ROWS = 128
HD = 128
JOIN = 4
SPAN = JOIN * ROWS
CTX, TP = 64, 8
GROUPS = CTX // JOIN
CAP = 4 * JOIN
SLOTS = GROUPS * CAP
ARRIVE = CTX * CAP
WIDE = 3 * HD


def dot(a, b, precision=None):
    return jnp.dot(a, b, preferred_element_type=F32, precision=precision)


def dot_nt(a, b, precision=None):
    return lax.dot_general(a, b, (((1,), (1,)), ((), ())), preferred_element_type=F32, precision=precision)


def dot_tn(a, b):
    return lax.dot_general(a, b, (((0,), (0,)), ((), ())), preferred_element_type=F32)


def iota(shape, dim):
    return lax.broadcasted_iota(I32, shape, dim)


def onehot(condition):
    return jnp.where(condition, 1.0, 0.0).astype(BF16)


def column(row):
    return jnp.broadcast_to(row, (ROWS, ROWS)).T


def kernel(
    pos_hbm, len_hbm, rate_hbm, gain_hbm, q_hbm, k_hbm, v_hbm, go_hbm,
    nrm_out, dq_out, got, give_out,
    pos_ref, len_ref, rate_ref, gain_ref, q_ref, k_ref, v_ref, go_ref, lsem,
    snd, rcv, sndq, snd2, pall, u_ref, ut_ref, w_ref, ends, qx, kx, vx, gox, att, attx, dob, pb, dpb,
    nrm_ref, dq_ref, give_ref, rcvq, state, state_in, back, back_in, part, parts, inv_ref, ssem, rsem, known,
):
    c, t = lax.axis_index("ctx"), lax.axis_index("tp")
    grp, k = c // JOIN, lax.rem(c, JOIN)
    own_cols = pl.ds(pl.multiple_of(k * HD, HD), HD)

    loads = [
        pltpu.make_async_copy(src, dst, lsem.at[i])
        for i, (src, dst) in enumerate(
            (
                (pos_hbm, pos_ref), (k_hbm, k_ref), (v_hbm, v_ref), (q_hbm, q_ref),
                (len_hbm, len_ref), (rate_hbm, rate_ref), (gain_hbm, gain_ref), (go_hbm, go_ref),
            )
        )
    ]
    for load in loads:
        load.start()
    own_y, own_z = c // 16, lax.rem(c, 16)

    def step_to(dy, dz):
        return lax.rem(own_y + dy, 4) * 16 + lax.rem(own_z + dz, 16)

    def peer(f):
        turn = f // 4
        h = (turn + 1) // 2
        return step_to(lax.rem(f, 4), jnp.where(lax.rem(turn, 2) == 1, h, 16 - h))

    barrier = pltpu.get_barrier_semaphore()
    near = 12

    @pl.loop(1, near)
    def _(f):
        pl.semaphore_signal(barrier, inc=1, device_id={"ctx": peer(f)}, device_id_type=MESH)

    @pl.loop(1, TP)
    def _(d):
        pl.semaphore_signal(barrier, inc=1, device_id={"tp": lax.rem(t + d, TP)}, device_id_type=MESH)

    def tell(reach, i):
        for j, dz in enumerate((16 - reach, reach)):
            pl.semaphore_signal(known.at[2 * i + j], inc=1, device_id={"ctx": step_to(0, dz)}, device_id_type=MESH)

    def learn(i):
        for j in range(2):
            pl.semaphore_wait(known.at[2 * i + j], 1)

    def remote(src, dst, index, **where):
        return pltpu.make_async_remote_copy(
            src_ref=src, dst_ref=dst, send_sem=ssem.at[index], recv_sem=rsem.at[index],
            device_id=where, device_id_type=MESH,
        )

    def wait(ref, sems, index):
        pltpu.make_async_copy(ref, ref, sems.at[index]).wait()

    loads[0].wait()
    pos = pos_ref[...]
    posr = jnp.broadcast_to(pos, (ROWS, ROWS))
    posc = posr.T
    gr, gc = posr >> 9, posc >> 9
    ri, ci = iota((ROWS, ROWS), 0), iota((ROWS, ROWS), 1)
    same = gr == gc
    rank_row = jnp.sum(jnp.where(same & (ri < ci), 1, 0), axis=0, keepdims=True)
    rank_col = jnp.sum(jnp.where(same & (ci < ri), 1, 0), axis=1, keepdims=True)
    slot_row = gr[:1] * CAP + rank_row
    slot_col = gc[:, :1] * CAP + rank_col
    pick = onehot(iota((SLOTS, ROWS), 0) == slot_row)

    def spread(ref, part_index):
        moved = dot(pick, ref[...]).astype(BF16)
        for h in range(JOIN):
            snd[:, h, :, part_index * HD : (part_index + 1) * HD] = moved[:, h * HD : (h + 1) * HD].reshape(
                GROUPS, CAP, HD
            )

    def send_rows(f, lo, n, index):
        p = peer(f)
        remote(
            snd.at[p // JOIN, lax.rem(p, JOIN), :, pl.ds(lo, n)],
            rcv.at[pl.ds(c * CAP, CAP), pl.ds(lo, n)],
            index, ctx=p,
        ).start()

    def send_stage(first, last):
        @pl.loop((first + 3) // 4, last // 4)
        def _(turn):
            remote(pos_ref, pall.at[pl.ds(c, 1)], 0, ctx=peer(4 * turn)).start()

        @pl.loop(first, last)
        def _(i):
            send_rows(last - 1 + first - i, 0, 2 * HD, 1)

    pl.semaphore_wait(barrier, near - 1 + TP - 1)
    tell(1, 0)
    for i, ref in enumerate((k_ref, v_ref)):
        loads[i + 1].wait()
        spread(ref, i)
    send_stage(1, near)
    learn(0)
    tell(2, 1)
    send_stage(near, 20)
    learn(1)
    tell(4, 2)

    @pl.loop(1, TP)
    def _(d):
        pl.semaphore_signal(known.at[6], inc=1, device_id={"tp": lax.rem(t + d, TP)}, device_id_type=MESH)

    send_stage(20, 36)
    loads[3].wait()
    spread(q_ref, 2)
    learn(2)
    send_stage(36, CTX)

    @pl.loop(1, CTX)
    def _(i):
        send_rows(CTX - i, 2 * HD, HD, 2)

    def mates(fn):
        for d in range(1, JOIN):
            m = lax.rem(k + d, JOIN)
            fn(m, grp * JOIN + m)

    rcv[pl.ds(c * CAP, CAP)] = snd[grp, k]
    pall[pl.ds(c, 1)] = pos
    give_ref[...] = onehot(iota((ROWS, SLOTS), 1) == slot_col)
    stores = [pltpu.make_async_copy(give_ref, give_out, lsem.at[8])]
    stores[0].start()
    for load in loads[4:]:
        load.wait()
    gox[pl.ds(k * ROWS, ROWS)] = go_ref[:, own_cols]

    rate = rate_ref[k]
    start = grp * SPAN
    here = iota((1, SPAN), 1) + start
    doc_row = jnp.full((1, SPAN), -1, I32)
    offset = jnp.int32(0)
    doc_prev, doc_next = jnp.int32(-1), jnp.int32(-1)
    doc_first, doc_last = jnp.int32(-1), jnp.int32(-1)
    for d in range(len_ref.shape[0]):
        doc_row += jnp.where(offset <= here, 1, 0)
        doc_prev += jnp.where(offset <= start - 1, 1, 0)
        doc_first += jnp.where(offset <= start, 1, 0)
        doc_last += jnp.where(offset <= start + SPAN - 1, 1, 0)
        doc_next += jnp.where(offset <= start + SPAN, 1, 0)
        offset += len_ref[d]
    doc_next = jnp.where(grp == GROUPS - 1, -2, doc_next)
    for i in range(JOIN):
        rows = slice(i * ROWS, (i + 1) * ROWS)
        doc_col = column(doc_row[:, rows])
        for j in range(i + 1):
            gap = (ri - ci) + (i - j) * ROWS
            kept = doc_col == doc_row[:, j * ROWS : (j + 1) * ROWS]
            if i == j:
                kept = kept & (gap >= 0)
            decay = jnp.exp(-rate * jnp.maximum(gap, 0).astype(F32))
            w_ref[rows, j * ROWS : (j + 1) * ROWS] = jnp.where(kept, decay, 0.0)
        at = (ri + i * ROWS).astype(F32)
        ends[0, rows] = jnp.where(doc_col == doc_prev, jnp.exp(-rate * (at + 1.0)), 0.0)
        ends[1, rows] = jnp.where(doc_col == doc_next, jnp.exp(-rate * (SPAN - at)), 0.0)
        ends[2, rows] = jnp.where(doc_col == doc_last, jnp.exp(-rate * (SPAN - 1.0 - at)), 0.0)
        ends[3, rows] = jnp.where(doc_col == doc_first, jnp.exp(-rate * at), 0.0)

    wait(pall.at[pl.ds(0, 15)], rsem, 0)
    own_line = pall.at[pl.ds(pl.multiple_of(own_y * 16, 16), 16)]
    for d in range(1, 4):
        remote(own_line, own_line, 9, ctx=lax.rem(own_y + d, 4) * 16 + own_z).start()
    wait(pall.at[pl.ds(0, 48)], rsem, 9)
    everywhere = pall[...]
    ours = everywhere >> 9 == grp
    rank = dot(onehot(ours), onehot(ri < ci))
    place = (everywhere & (SPAN - 1)).astype(F32) + 1.0
    places = jnp.zeros((CTX, ROWS), F32)
    for r in range(CAP):
        held = jnp.sum(jnp.where(ours & (rank == float(r)), place, 0.0), axis=1, keepdims=True)
        places = jnp.where(iota((CTX, ROWS), 1) == r, held, places)
    tile = jnp.where(lax.rem(iota((ROWS, ARRIVE), 1), CAP) == iota((ROWS, ARRIVE), 0), 1.0, 0.0)
    owner = iota((CTX, ARRIVE), 1) // CAP == iota((CTX, ARRIVE), 0)
    place_row = jnp.sum(jnp.where(owner, dot(places, tile, HIGHEST), 0.0), axis=0, keepdims=True) - 1.0
    place_row = place_row.astype(I32)
    for i in range(JOIN):
        rows = slice(i * ROWS, (i + 1) * ROWS)
        u_ref[rows] = onehot(iota((ROWS, ARRIVE), 0) + i * ROWS == place_row)
    for j in range(ARRIVE // ROWS):
        cols = slice(j * ROWS, (j + 1) * ROWS)
        place_col = column(place_row[:, cols])
        for i in range(JOIN):
            ut_ref[cols, i * ROWS : (i + 1) * ROWS] = onehot(place_col == ci + i * ROWS)

    wait(rcv.at[pl.ds(0, ARRIVE - CAP), pl.ds(0, 2 * HD)], rsem, 1)
    kv = dot(u_ref[...], rcv[:, : 2 * HD]).astype(BF16)
    kx[...] = kv[:, :HD]
    vx[...] = kv[:, HD:]
    state[...] = dot_tn((kx[...].astype(F32) * ends[2]).astype(BF16), vx[...]).astype(BF16)
    remote(state, state_in, 4, ctx=lax.rem(c + JOIN, CTX)).start()
    mates(
        lambda m, p: remote(
            go_ref.at[:, pl.ds(pl.multiple_of(m * HD, HD), HD)], gox.at[pl.ds(k * ROWS, ROWS)], 3, ctx=p
        ).start()
    )

    wait(rcv.at[pl.ds(0, ARRIVE - CAP), pl.ds(2 * HD, HD)], rsem, 2)
    qx[...] = dot(u_ref[...], rcv[:, 2 * HD :]).astype(BF16)
    for i in range(JOIN):
        rows, n = slice(i * ROWS, (i + 1) * ROWS), (i + 1) * ROWS
        pb[rows, :n] = (dot_nt(qx[rows], kx[:n]) * w_ref[rows, :n]).astype(BF16)
    wait(state_in, rsem, 4)
    gain = gain_ref[:, own_cols]
    ones = jnp.ones((8, HD), BF16)

    def row_sums(x):
        high = x.astype(BF16)
        low = (x - high.astype(F32)).astype(BF16)
        return (dot_nt(ones, high) + dot_nt(ones, low))[:1]

    for i in range(JOIN):
        rows, n = slice(i * ROWS, (i + 1) * ROWS), (i + 1) * ROWS
        entered = (qx[rows].astype(F32) * ends[0, rows]).astype(BF16)
        a = (dot(pb[rows, :n], vx[:n]) + dot(entered, state_in[...])).astype(BF16)
        att[rows] = a
        a = a.astype(F32)
        part[i : i + 1] = row_sums(a * a)
    wait(gox.at[pl.ds(0, SPAN - ROWS)], rsem, 3)
    for i in range(JOIN):
        rows = slice(i * ROWS, (i + 1) * ROWS)
        g = gox[rows].astype(F32) * gain
        part[JOIN + i : JOIN + i + 1] = row_sums(g * att[rows].astype(F32))

    pl.semaphore_wait(known.at[6], TP - 1)

    @pl.loop(1, JOIN * TP)
    def _(i):
        m = lax.rem(k + i // TP, JOIN)
        remote(part, parts.at[k * TP + t], 5, ctx=grp * JOIN + m, tp=lax.rem(t + i, TP)).start()

    mates(
        lambda m, p: remote(
            att.at[pl.ds(pl.multiple_of(m * ROWS, ROWS), ROWS)], attx.at[:, own_cols], 7, ctx=p
        ).start()
    )
    attx[:, own_cols] = att[pl.ds(pl.multiple_of(k * ROWS, ROWS), ROWS)]
    parts[k * TP + t] = part[...]
    wait(parts.at[pl.ds(0, JOIN * TP - 1)], rsem, 5)
    total = jnp.sum(parts[...], axis=0)
    width = float(HD * JOIN * TP)
    inverse = lax.rsqrt(total[:JOIN] / width + EPSILON)
    coef = inverse * inverse * inverse * total[JOIN:] / width
    inv_ref[...] = inverse

    carried = jnp.zeros((HD, HD), F32)
    for i in range(JOIN):
        rows = slice(i * ROWS, (i + 1) * ROWS)
        inv, cf = column(inverse[i : i + 1]), column(coef[i : i + 1])
        a = att[rows].astype(F32)
        g = gox[rows].astype(F32) * gain
        d_o = (inv * g - a * cf).astype(BF16)
        dob[rows] = d_o
        carried += dot_tn((qx[rows].astype(F32) * ends[3, rows]).astype(BF16), d_o)
    back[...] = carried.astype(BF16)
    remote(back, back_in, 8, ctx=lax.rem(c + CTX - JOIN, CTX)).start()

    def send_back(src, dst, index):
        @pl.loop(1, CTX)
        def _(d):
            p = peer(CTX - d)
            remote(src.at[pl.ds(p * CAP, CAP)], dst.at[k, pl.ds(grp * CAP, CAP)], index, ctx=p).start()

    dq = []
    for i in range(JOIN):
        rows, n = slice(i * ROWS, (i + 1) * ROWS), (i + 1) * ROWS
        dp = (dot_nt(dob[rows], vx[:n]) * w_ref[rows, :n]).astype(BF16)
        dpb[rows, :n] = dp
        entered = (dob[rows].astype(F32) * ends[0, rows]).astype(BF16)
        dq.append((dot(dp, kx[:n]) + dot_nt(entered, state_in[...])).astype(BF16))
    sndq[...] = dot(ut_ref[...], jnp.concatenate(dq, axis=0)).astype(BF16)
    send_back(sndq, rcvq, 10)
    rcvq[k, pl.ds(grp * CAP, CAP)] = sndq[pl.ds(c * CAP, CAP)]

    wait(back_in, rsem, 8)
    dk, dv = [], []
    for j in range(JOIN):
        cols, low = slice(j * ROWS, (j + 1) * ROWS), j * ROWS
        leave = ends[1, cols]
        value = (vx[cols].astype(F32) * leave).astype(BF16)
        key = (kx[cols].astype(F32) * leave).astype(BF16)
        dk.append((dot_tn(dpb[low:, cols], qx[low:]) + dot_nt(value, back_in[...])).astype(BF16))
        dv.append((dot_tn(pb[low:, cols], dob[low:]) + dot(key, back_in[...])).astype(BF16))
    both = jnp.concatenate([jnp.concatenate(dk, axis=0), jnp.concatenate(dv, axis=0)], axis=1)
    snd2[...] = dot(ut_ref[...], both).astype(BF16)
    send_back(snd2, got, 11)
    stores.append(
        pltpu.make_async_copy(snd2.at[pl.ds(c * CAP, CAP)], got.at[k, pl.ds(grp * CAP, CAP)], lsem.at[9])
    )
    stores[-1].start()

    wait(att.at[pl.ds(0, SPAN - ROWS)], rsem, 7)
    inv = column(inv_ref[pl.ds(k, 1)])
    for h in range(JOIN):
        cols = slice(h * HD, (h + 1) * HD)
        nrm_ref[:, cols] = (attx[:, cols].astype(F32) * inv * gain_ref[:, cols]).astype(BF16)
    stores.append(pltpu.make_async_copy(nrm_ref, nrm_out, lsem.at[10]))
    stores[-1].start()

    wait(sndq.at[pl.ds(0, ARRIVE - CAP)], rsem, 10)
    for h in range(JOIN):
        dq_ref[:, h * HD : (h + 1) * HD] = dot(give_ref[...], rcvq[h]).astype(BF16)
    stores.append(pltpu.make_async_copy(dq_ref, dq_out, lsem.at[11]))
    stores[-1].start()
    wait(snd2.at[pl.ds(0, ARRIVE - CAP)], rsem, 11)

    wait(pall.at[pl.ds(0, 15)], ssem, 0)
    wait(rcv.at[pl.ds(0, ARRIVE - CAP), pl.ds(0, 2 * HD)], ssem, 1)
    wait(rcv.at[pl.ds(0, ARRIVE - CAP), pl.ds(2 * HD, HD)], ssem, 2)
    wait(gox.at[pl.ds(0, SPAN - ROWS)], ssem, 3)
    wait(state, ssem, 4)
    wait(parts.at[pl.ds(0, JOIN * TP - 1)], ssem, 5)
    wait(att.at[pl.ds(0, SPAN - ROWS)], ssem, 7)
    wait(back, ssem, 8)
    wait(pall.at[pl.ds(0, 48)], ssem, 9)
    wait(sndq.at[pl.ds(0, ARRIVE - CAP)], ssem, 10)
    wait(snd2.at[pl.ds(0, ARRIVE - CAP)], ssem, 11)
    for store in stores:
        store.wait()


def finish(nrm, dq, got, give, nrm_out, dq_out, dk_out, dv_out, *scratch):
    nrm_ref, dq_ref, got_ref, give_ref, dk_ref, dv_ref, sem = scratch
    loads = [
        pltpu.make_async_copy(src, dst, sem.at[i])
        for i, (src, dst) in enumerate(((give, give_ref), (got, got_ref), (nrm, nrm_ref), (dq, dq_ref)))
    ]
    stores = [
        pltpu.make_async_copy(src, dst, sem.at[4 + i])
        for i, (src, dst) in enumerate(((dk_ref, dk_out), (dv_ref, dv_out), (nrm_ref, nrm_out), (dq_ref, dq_out)))
    ]
    for load in loads:
        load.start()
    for load in loads[:2]:
        load.wait()
    for i, ref in enumerate((dk_ref, dv_ref)):
        for h in range(JOIN):
            moved = dot(give_ref[...], got_ref[h, :, i * HD : (i + 1) * HD])
            ref[:, h * HD : (h + 1) * HD] = moved.astype(BF16)
        stores[i].start()
    for load, store in zip(loads[2:], stores[2:]):
        load.wait()
        store.start()
    for store in stores:
        store.wait()


def body(query_rows, key_rows, value_rows, position, lengths, decay_rates, norm_gain, grad_output):
    hbm = pl.BlockSpec(memory_space=pltpu.HBM)
    shape = jax.ShapeDtypeStruct(query_rows.shape, BF16)
    held = pltpu.VMEM(query_rows.shape, BF16)
    kept = pl.pallas_call(
        kernel,
        out_shape=(
            shape, shape,
            jax.ShapeDtypeStruct((JOIN, SLOTS, 2 * HD), BF16), jax.ShapeDtypeStruct((ROWS, SLOTS), BF16),
        ),
        in_specs=[hbm] * 8,
        out_specs=(hbm,) * 4,
        scratch_shapes=[
            pltpu.VMEM((1, ROWS), I32),
            pltpu.SMEM(lengths.shape, I32),
            pltpu.SMEM(decay_rates.shape, F32),
            pltpu.VMEM((1, JOIN * HD), F32),
            held, held, held, held,
            pltpu.SemaphoreType.DMA((12,)),
            pltpu.VMEM((GROUPS, JOIN, CAP, WIDE), BF16),
            pltpu.VMEM((ARRIVE, WIDE), BF16),
            pltpu.VMEM((ARRIVE, HD), BF16),
            pltpu.VMEM((ARRIVE, 2 * HD), BF16),
            pltpu.VMEM((CTX, ROWS), I32),
            pltpu.VMEM((SPAN, ARRIVE), BF16),
            pltpu.VMEM((ARRIVE, SPAN), BF16),
            pltpu.VMEM((SPAN, SPAN), F32),
            pltpu.VMEM((4, SPAN, HD), F32),
            pltpu.VMEM((SPAN, HD), BF16),
            pltpu.VMEM((SPAN, HD), BF16),
            pltpu.VMEM((SPAN, HD), BF16),
            pltpu.VMEM((SPAN, HD), BF16),
            pltpu.VMEM((SPAN, HD), BF16),
            held,
            pltpu.VMEM((SPAN, HD), BF16),
            pltpu.VMEM((SPAN, SPAN), BF16),
            pltpu.VMEM((SPAN, SPAN), BF16),
            held, held,
            pltpu.VMEM((ROWS, SLOTS), BF16),
            pltpu.VMEM((JOIN, SLOTS, HD), BF16),
            pltpu.VMEM((HD, HD), BF16),
            pltpu.VMEM((HD, HD), BF16),
            pltpu.VMEM((HD, HD), BF16),
            pltpu.VMEM((HD, HD), BF16),
            pltpu.VMEM((2 * JOIN, ROWS), F32),
            pltpu.VMEM((JOIN * TP, 2 * JOIN, ROWS), F32),
            pltpu.VMEM((JOIN, ROWS), F32),
            pltpu.SemaphoreType.DMA((12,)),
            pltpu.SemaphoreType.DMA((12,)),
            pltpu.SemaphoreType.REGULAR((7,)),
        ],
        compiler_params=pltpu.CompilerParams(
            collective_id=0, has_side_effects=True, vmem_limit_bytes=60 << 20
        ),
        name="lightning",
    )(
        position.reshape(1, ROWS), lengths, decay_rates, norm_gain.reshape(1, -1),
        query_rows, key_rows, value_rows, grad_output,
    )
    return pl.pallas_call(
        finish,
        out_shape=(shape,) * 4,
        in_specs=[hbm] * 4,
        out_specs=(hbm,) * 4,
        scratch_shapes=[
            held, held, pltpu.VMEM((JOIN, SLOTS, 2 * HD), BF16), pltpu.VMEM((ROWS, SLOTS), BF16),
            held, held, pltpu.SemaphoreType.DMA((8,)),
        ],
        compiler_params=pltpu.CompilerParams(vmem_limit_bytes=60 << 20),
        name="finish",
    )(*kept)


def solution(mesh):
    rows, specs = P("ctx", "tp"), (P("ctx", "tp"),) * 4
    return jax.shard_map(
        body,
        mesh=mesh,
        in_specs=(rows, rows, rows, P("ctx"), P(), P("tp"), P("tp"), rows),
        out_specs=specs,
        check_vma=False,
    )
```

```python
import jax
import jax.numpy as jnp
from jax import lax
from jax.experimental import pallas as pl
from jax.experimental.pallas import tpu as pltpu
from jax.sharding import PartitionSpec as P

MESH = pl.DeviceIdType.MESH
F32, BF16, I32 = jnp.float32, jnp.bfloat16, jnp.int32
HIGHEST = lax.Precision.HIGHEST
EPSILON = 1e-05
ROWS = 128
HD = 128
JOIN = 4
SPAN = JOIN * ROWS
CTX, TP = 64, 8
GROUPS = CTX // JOIN
CAP = 4 * JOIN
SLOTS = GROUPS * CAP
ARRIVE = CTX * CAP
WIDE = 3 * HD


def dot(a, b, precision=None):
    return jnp.dot(a, b, preferred_element_type=F32, precision=precision)


def dot_nt(a, b, precision=None):
    return lax.dot_general(a, b, (((1,), (1,)), ((), ())), preferred_element_type=F32, precision=precision)


def dot_tn(a, b):
    return lax.dot_general(a, b, (((0,), (0,)), ((), ())), preferred_element_type=F32)


def iota(shape, dim):
    return lax.broadcasted_iota(I32, shape, dim)


def onehot(condition):
    return jnp.where(condition, 1.0, 0.0).astype(BF16)


def column(row):
    return jnp.broadcast_to(row, (ROWS, ROWS)).T


def kernel(
    pos_hbm, len_hbm, rate_hbm, gain_hbm, q_hbm, k_hbm, v_hbm, go_hbm,
    nrm_out, dq_out, got, give_out,
    pos_ref, len_ref, rate_ref, gain_ref, q_ref, k_ref, v_ref, go_ref, lsem,
    snd, rcv, sndq, snd2, pall, u_ref, ut_ref, w_ref, ends, qx, kx, vx, gox, att, attx, dob, pb, dpb,
    nrm_ref, dq_ref, give_ref, rcvq, state, state_in, back, back_in, part, parts, inv_ref, ssem, rsem, known,
):
    c, t = lax.axis_index("ctx"), lax.axis_index("tp")
    grp, k = c // JOIN, lax.rem(c, JOIN)
    own_cols = pl.ds(pl.multiple_of(k * HD, HD), HD)

    loads = [
        pltpu.make_async_copy(src, dst, lsem.at[i])
        for i, (src, dst) in enumerate(
            (
                (pos_hbm, pos_ref), (k_hbm, k_ref), (v_hbm, v_ref), (q_hbm, q_ref),
                (len_hbm, len_ref), (rate_hbm, rate_ref), (gain_hbm, gain_ref), (go_hbm, go_ref),
            )
        )
    ]
    for load in loads:
        load.start()
    own_y, own_z = c // 16, lax.rem(c, 16)

    def step_to(dy, dz):
        return lax.rem(own_y + dy, 4) * 16 + lax.rem(own_z + dz, 16)

    def peer(f):
        turn = f // 4
        h = (turn + 1) // 2
        return step_to(lax.rem(f, 4), jnp.where(lax.rem(turn, 2) == 1, h, 16 - h))

    barrier = pltpu.get_barrier_semaphore()
    near = 12

    @pl.loop(1, near)
    def _(f):
        pl.semaphore_signal(barrier, inc=1, device_id={"ctx": peer(f)}, device_id_type=MESH)

    @pl.loop(1, TP)
    def _(d):
        pl.semaphore_signal(barrier, inc=1, device_id={"tp": lax.rem(t + d, TP)}, device_id_type=MESH)

    def tell(reach, i):
        for j, dz in enumerate((16 - reach, reach)):
            pl.semaphore_signal(known.at[2 * i + j], inc=1, device_id={"ctx": step_to(0, dz)}, device_id_type=MESH)

    def learn(i):
        for j in range(2):
            pl.semaphore_wait(known.at[2 * i + j], 1)

    def remote(src, dst, index, **where):
        return pltpu.make_async_remote_copy(
            src_ref=src, dst_ref=dst, send_sem=ssem.at[index], recv_sem=rsem.at[index],
            device_id=where, device_id_type=MESH,
        )

    def wait(ref, sems, index):
        pltpu.make_async_copy(ref, ref, sems.at[index]).wait()

    loads[0].wait()
    pos = pos_ref[...]
    posr = jnp.broadcast_to(pos, (ROWS, ROWS))
    posc = posr.T
    gr, gc = posr >> 9, posc >> 9
    ri, ci = iota((ROWS, ROWS), 0), iota((ROWS, ROWS), 1)
    same = gr == gc
    rank_row = jnp.sum(jnp.where(same & (ri < ci), 1, 0), axis=0, keepdims=True)
    rank_col = jnp.sum(jnp.where(same & (ci < ri), 1, 0), axis=1, keepdims=True)
    slot_row = gr[:1] * CAP + rank_row
    slot_col = gc[:, :1] * CAP + rank_col
    pick = onehot(iota((SLOTS, ROWS), 0) == slot_row)

    def spread(ref, part_index):
        moved = dot(pick, ref[...]).astype(BF16)
        for h in range(JOIN):
            snd[:, h, :, part_index * HD : (part_index + 1) * HD] = moved[:, h * HD : (h + 1) * HD].reshape(
                GROUPS, CAP, HD
            )

    def send_rows(f, lo, n, index):
        p = peer(f)
        remote(
            snd.at[p // JOIN, lax.rem(p, JOIN), :, pl.ds(lo, n)],
            rcv.at[pl.ds(c * CAP, CAP), pl.ds(lo, n)],
            index, ctx=p,
        ).start()

    def send_stage(first, last):
        @pl.loop((first + 3) // 4, last // 4)
        def _(turn):
            remote(pos_ref, pall.at[pl.ds(c, 1)], 0, ctx=peer(4 * turn)).start()

        @pl.loop(first, last)
        def _(i):
            send_rows(last - 1 + first - i, 0, 2 * HD, 1)

    pl.semaphore_wait(barrier, near - 1 + TP - 1)
    tell(1, 0)
    for i, ref in enumerate((k_ref, v_ref)):
        loads[i + 1].wait()
        spread(ref, i)
    send_stage(1, near)
    learn(0)
    tell(2, 1)
    send_stage(near, 20)
    learn(1)
    tell(4, 2)

    @pl.loop(1, TP)
    def _(d):
        pl.semaphore_signal(known.at[6], inc=1, device_id={"tp": lax.rem(t + d, TP)}, device_id_type=MESH)

    send_stage(20, 36)
    loads[3].wait()
    spread(q_ref, 2)
    learn(2)
    send_stage(36, CTX)

    @pl.loop(1, CTX)
    def _(i):
        send_rows(CTX - i, 2 * HD, HD, 2)

    def mates(fn):
        for d in range(1, JOIN):
            m = lax.rem(k + d, JOIN)
            fn(m, grp * JOIN + m)

    rcv[pl.ds(c * CAP, CAP)] = snd[grp, k]
    pall[pl.ds(c, 1)] = pos
    give_ref[...] = onehot(iota((ROWS, SLOTS), 1) == slot_col)
    stores = [pltpu.make_async_copy(give_ref, give_out, lsem.at[8])]
    stores[0].start()
    for load in loads[4:]:
        load.wait()
    gox[pl.ds(k * ROWS, ROWS)] = go_ref[:, own_cols]

    rate = rate_ref[k]
    start = grp * SPAN
    here = iota((1, SPAN), 1) + start
    doc_row = jnp.full((1, SPAN), -1, I32)
    offset = jnp.int32(0)
    doc_prev, doc_next = jnp.int32(-1), jnp.int32(-1)
    doc_first, doc_last = jnp.int32(-1), jnp.int32(-1)
    for d in range(len_ref.shape[0]):
        doc_row += jnp.where(offset <= here, 1, 0)
        doc_prev += jnp.where(offset <= start - 1, 1, 0)
        doc_first += jnp.where(offset <= start, 1, 0)
        doc_last += jnp.where(offset <= start + SPAN - 1, 1, 0)
        doc_next += jnp.where(offset <= start + SPAN, 1, 0)
        offset += len_ref[d]
    doc_next = jnp.where(grp == GROUPS - 1, -2, doc_next)
    for i in range(JOIN):
        rows = slice(i * ROWS, (i + 1) * ROWS)
        doc_col = column(doc_row[:, rows])
        for j in range(i + 1):
            gap = (ri - ci) + (i - j) * ROWS
            kept = doc_col == doc_row[:, j * ROWS : (j + 1) * ROWS]
            if i == j:
                kept = kept & (gap >= 0)
            decay = jnp.exp(-rate * jnp.maximum(gap, 0).astype(F32))
            w_ref[rows, j * ROWS : (j + 1) * ROWS] = jnp.where(kept, decay, 0.0)
        at = (ri + i * ROWS).astype(F32)
        ends[0, rows] = jnp.where(doc_col == doc_prev, jnp.exp(-rate * (at + 1.0)), 0.0)
        ends[1, rows] = jnp.where(doc_col == doc_next, jnp.exp(-rate * (SPAN - at)), 0.0)
        ends[2, rows] = jnp.where(doc_col == doc_last, jnp.exp(-rate * (SPAN - 1.0 - at)), 0.0)
        ends[3, rows] = jnp.where(doc_col == doc_first, jnp.exp(-rate * at), 0.0)

    wait(pall.at[pl.ds(0, 15)], rsem, 0)
    own_line = pall.at[pl.ds(pl.multiple_of(own_y * 16, 16), 16)]
    for d in range(1, 4):
        remote(own_line, own_line, 9, ctx=lax.rem(own_y + d, 4) * 16 + own_z).start()
    wait(pall.at[pl.ds(0, 48)], rsem, 9)
    everywhere = pall[...]
    ours = everywhere >> 9 == grp
    rank = dot(onehot(ours), onehot(ri < ci))
    place = (everywhere & (SPAN - 1)).astype(F32) + 1.0
    places = jnp.zeros((CTX, ROWS), F32)
    for r in range(CAP):
        held = jnp.sum(jnp.where(ours & (rank == float(r)), place, 0.0), axis=1, keepdims=True)
        places = jnp.where(iota((CTX, ROWS), 1) == r, held, places)
    tile = jnp.where(lax.rem(iota((ROWS, ARRIVE), 1), CAP) == iota((ROWS, ARRIVE), 0), 1.0, 0.0)
    owner = iota((CTX, ARRIVE), 1) // CAP == iota((CTX, ARRIVE), 0)
    place_row = jnp.sum(jnp.where(owner, dot(places, tile, HIGHEST), 0.0), axis=0, keepdims=True) - 1.0
    place_row = place_row.astype(I32)
    for i in range(JOIN):
        rows = slice(i * ROWS, (i + 1) * ROWS)
        u_ref[rows] = onehot(iota((ROWS, ARRIVE), 0) + i * ROWS == place_row)
    for j in range(ARRIVE // ROWS):
        cols = slice(j * ROWS, (j + 1) * ROWS)
        place_col = column(place_row[:, cols])
        for i in range(JOIN):
            ut_ref[cols, i * ROWS : (i + 1) * ROWS] = onehot(place_col == ci + i * ROWS)

    wait(rcv.at[pl.ds(0, ARRIVE - CAP), pl.ds(0, 2 * HD)], rsem, 1)
    kv = dot(u_ref[...], rcv[:, : 2 * HD]).astype(BF16)
    kx[...] = kv[:, :HD]
    vx[...] = kv[:, HD:]
    state[...] = dot_tn((kx[...].astype(F32) * ends[2]).astype(BF16), vx[...]).astype(BF16)
    for i in range(0, HD, 16):
        remote(state.at[pl.ds(i, 16)], state_in.at[pl.ds(i, 16)], 4, ctx=lax.rem(c + JOIN, CTX)).start()
    mates(
        lambda m, p: remote(
            go_ref.at[:, pl.ds(pl.multiple_of(m * HD, HD), HD)], gox.at[pl.ds(k * ROWS, ROWS)], 3, ctx=p
        ).start()
    )

    wait(rcv.at[pl.ds(0, ARRIVE - CAP), pl.ds(2 * HD, HD)], rsem, 2)
    qx[...] = dot(u_ref[...], rcv[:, 2 * HD :]).astype(BF16)
    for i in range(JOIN):
        rows, n = slice(i * ROWS, (i + 1) * ROWS), (i + 1) * ROWS
        pb[rows, :n] = (dot_nt(qx[rows], kx[:n]) * w_ref[rows, :n]).astype(BF16)
    wait(state_in, rsem, 4)
    gain = gain_ref[:, own_cols]
    ones = jnp.ones((8, HD), BF16)

    def row_sums(x):
        high = x.astype(BF16)
        low = (x - high.astype(F32)).astype(BF16)
        return (dot_nt(ones, high) + dot_nt(ones, low))[:1]

    for i in range(JOIN):
        rows, n = slice(i * ROWS, (i + 1) * ROWS), (i + 1) * ROWS
        entered = (qx[rows].astype(F32) * ends[0, rows]).astype(BF16)
        a = (dot(pb[rows, :n], vx[:n]) + dot(entered, state_in[...])).astype(BF16)
        att[rows] = a
        a = a.astype(F32)
        part[i : i + 1] = row_sums(a * a)
    wait(gox.at[pl.ds(0, SPAN - ROWS)], rsem, 3)
    for i in range(JOIN):
        rows = slice(i * ROWS, (i + 1) * ROWS)
        g = gox[rows].astype(F32) * gain
        part[JOIN + i : JOIN + i + 1] = row_sums(g * att[rows].astype(F32))

    pl.semaphore_wait(known.at[6], TP - 1)

    @pl.loop(1, JOIN * TP)
    def _(i):
        m = lax.rem(k + i // TP, JOIN)
        remote(part, parts.at[k * TP + t], 5, ctx=grp * JOIN + m, tp=lax.rem(t + i, TP)).start()

    mates(
        lambda m, p: remote(
            att.at[pl.ds(pl.multiple_of(m * ROWS, ROWS), ROWS)], attx.at[:, own_cols], 7, ctx=p
        ).start()
    )
    attx[:, own_cols] = att[pl.ds(pl.multiple_of(k * ROWS, ROWS), ROWS)]
    parts[k * TP + t] = part[...]
    wait(parts.at[pl.ds(0, JOIN * TP - 1)], rsem, 5)
    total = jnp.sum(parts[...], axis=0)
    width = float(HD * JOIN * TP)
    inverse = lax.rsqrt(total[:JOIN] / width + EPSILON)
    coef = inverse * inverse * inverse * total[JOIN:] / width
    inv_ref[...] = inverse

    carried = jnp.zeros((HD, HD), F32)
    for i in range(JOIN):
        rows = slice(i * ROWS, (i + 1) * ROWS)
        inv, cf = column(inverse[i : i + 1]), column(coef[i : i + 1])
        a = att[rows].astype(F32)
        g = gox[rows].astype(F32) * gain
        d_o = (inv * g - a * cf).astype(BF16)
        dob[rows] = d_o
        carried += dot_tn((qx[rows].astype(F32) * ends[3, rows]).astype(BF16), d_o)
    back[...] = carried.astype(BF16)
    for i in range(0, HD, 16):
        remote(back.at[pl.ds(i, 16)], back_in.at[pl.ds(i, 16)], 8, ctx=lax.rem(c + CTX - JOIN, CTX)).start()

    def send_back(src, dst, index, early):
        def send(p):
            remote(src.at[pl.ds(p * CAP, CAP)], dst.at[k, pl.ds(grp * CAP, CAP)], index, ctx=p).start()

        @pl.loop(0, 4 * early)
        def _(i):
            p = lax.rem(own_y + i, 4) * 16 + i // 4
            pl.when(p != c)(lambda: send(p))

        @pl.loop(1, CTX)
        def _(d):
            p = peer(CTX - d)
            pl.when(lax.rem(p, 16) >= early)(lambda: send(p))

    dq = []
    for i in range(JOIN):
        rows, n = slice(i * ROWS, (i + 1) * ROWS), (i + 1) * ROWS
        dp = (dot_nt(dob[rows], vx[:n]) * w_ref[rows, :n]).astype(BF16)
        dpb[rows, :n] = dp
        entered = (dob[rows].astype(F32) * ends[0, rows]).astype(BF16)
        dq.append((dot(dp, kx[:n]) + dot_nt(entered, state_in[...])).astype(BF16))
    sndq[...] = dot(ut_ref[...], jnp.concatenate(dq, axis=0)).astype(BF16)
    send_back(sndq, rcvq, 10, 6)
    rcvq[k, pl.ds(grp * CAP, CAP)] = sndq[pl.ds(c * CAP, CAP)]

    wait(back_in, rsem, 8)
    dk, dv = [], []
    for j in range(JOIN):
        cols, low = slice(j * ROWS, (j + 1) * ROWS), j * ROWS
        leave = ends[1, cols]
        value = (vx[cols].astype(F32) * leave).astype(BF16)
        key = (kx[cols].astype(F32) * leave).astype(BF16)
        dk.append((dot_tn(dpb[low:, cols], qx[low:]) + dot_nt(value, back_in[...])).astype(BF16))
        dv.append((dot_tn(pb[low:, cols], dob[low:]) + dot(key, back_in[...])).astype(BF16))
    both = jnp.concatenate([jnp.concatenate(dk, axis=0), jnp.concatenate(dv, axis=0)], axis=1)
    snd2[...] = dot(ut_ref[...], both).astype(BF16)
    send_back(snd2, got, 11, 6)
    stores.append(
        pltpu.make_async_copy(snd2.at[pl.ds(c * CAP, CAP)], got.at[k, pl.ds(grp * CAP, CAP)], lsem.at[9])
    )
    stores[-1].start()

    wait(att.at[pl.ds(0, SPAN - ROWS)], rsem, 7)
    inv = column(inv_ref[pl.ds(k, 1)])
    for h in range(JOIN):
        cols = slice(h * HD, (h + 1) * HD)
        nrm_ref[:, cols] = (attx[:, cols].astype(F32) * inv * gain_ref[:, cols]).astype(BF16)
    stores.append(pltpu.make_async_copy(nrm_ref, nrm_out, lsem.at[10]))
    stores[-1].start()

    wait(sndq.at[pl.ds(0, ARRIVE - CAP)], rsem, 10)
    for h in range(JOIN):
        dq_ref[:, h * HD : (h + 1) * HD] = dot(give_ref[...], rcvq[h]).astype(BF16)
    stores.append(pltpu.make_async_copy(dq_ref, dq_out, lsem.at[11]))
    stores[-1].start()
    wait(snd2.at[pl.ds(0, ARRIVE - CAP)], rsem, 11)

    wait(pall.at[pl.ds(0, 15)], ssem, 0)
    wait(rcv.at[pl.ds(0, ARRIVE - CAP), pl.ds(0, 2 * HD)], ssem, 1)
    wait(rcv.at[pl.ds(0, ARRIVE - CAP), pl.ds(2 * HD, HD)], ssem, 2)
    wait(gox.at[pl.ds(0, SPAN - ROWS)], ssem, 3)
    wait(state, ssem, 4)
    wait(parts.at[pl.ds(0, JOIN * TP - 1)], ssem, 5)
    wait(att.at[pl.ds(0, SPAN - ROWS)], ssem, 7)
    wait(back, ssem, 8)
    wait(pall.at[pl.ds(0, 48)], ssem, 9)
    wait(sndq.at[pl.ds(0, ARRIVE - CAP)], ssem, 10)
    wait(snd2.at[pl.ds(0, ARRIVE - CAP)], ssem, 11)
    for store in stores:
        store.wait()


def finish(nrm, dq, got, give, nrm_out, dq_out, dk_out, dv_out, *scratch):
    nrm_ref, dq_ref, got_ref, give_ref, dk_ref, dv_ref, sem = scratch
    loads = [
        pltpu.make_async_copy(src, dst, sem.at[i])
        for i, (src, dst) in enumerate(((give, give_ref), (got, got_ref), (nrm, nrm_ref), (dq, dq_ref)))
    ]
    stores = [
        pltpu.make_async_copy(src, dst, sem.at[4 + i])
        for i, (src, dst) in enumerate(((dk_ref, dk_out), (dv_ref, dv_out), (nrm_ref, nrm_out), (dq_ref, dq_out)))
    ]
    for load in loads:
        load.start()
    for load in loads[:2]:
        load.wait()
    for i, ref in enumerate((dk_ref, dv_ref)):
        for h in range(JOIN):
            moved = dot(give_ref[...], got_ref[h, :, i * HD : (i + 1) * HD])
            ref[:, h * HD : (h + 1) * HD] = moved.astype(BF16)
        stores[i].start()
    for load, store in zip(loads[2:], stores[2:]):
        load.wait()
        store.start()
    for store in stores:
        store.wait()


def body(query_rows, key_rows, value_rows, position, lengths, decay_rates, norm_gain, grad_output):
    hbm = pl.BlockSpec(memory_space=pltpu.HBM)
    shape = jax.ShapeDtypeStruct(query_rows.shape, BF16)
    held = pltpu.VMEM(query_rows.shape, BF16)
    kept = pl.pallas_call(
        kernel,
        out_shape=(
            shape, shape,
            jax.ShapeDtypeStruct((JOIN, SLOTS, 2 * HD), BF16), jax.ShapeDtypeStruct((ROWS, SLOTS), BF16),
        ),
        in_specs=[hbm] * 8,
        out_specs=(hbm,) * 4,
        scratch_shapes=[
            pltpu.VMEM((1, ROWS), I32),
            pltpu.SMEM(lengths.shape, I32),
            pltpu.SMEM(decay_rates.shape, F32),
            pltpu.VMEM((1, JOIN * HD), F32),
            held, held, held, held,
            pltpu.SemaphoreType.DMA((12,)),
            pltpu.VMEM((GROUPS, JOIN, CAP, WIDE), BF16),
            pltpu.VMEM((ARRIVE, WIDE), BF16),
            pltpu.VMEM((ARRIVE, HD), BF16),
            pltpu.VMEM((ARRIVE, 2 * HD), BF16),
            pltpu.VMEM((CTX, ROWS), I32),
            pltpu.VMEM((SPAN, ARRIVE), BF16),
            pltpu.VMEM((ARRIVE, SPAN), BF16),
            pltpu.VMEM((SPAN, SPAN), F32),
            pltpu.VMEM((4, SPAN, HD), F32),
            pltpu.VMEM((SPAN, HD), BF16),
            pltpu.VMEM((SPAN, HD), BF16),
            pltpu.VMEM((SPAN, HD), BF16),
            pltpu.VMEM((SPAN, HD), BF16),
            pltpu.VMEM((SPAN, HD), BF16),
            held,
            pltpu.VMEM((SPAN, HD), BF16),
            pltpu.VMEM((SPAN, SPAN), BF16),
            pltpu.VMEM((SPAN, SPAN), BF16),
            held, held,
            pltpu.VMEM((ROWS, SLOTS), BF16),
            pltpu.VMEM((JOIN, SLOTS, HD), BF16),
            pltpu.VMEM((HD, HD), BF16),
            pltpu.VMEM((HD, HD), BF16),
            pltpu.VMEM((HD, HD), BF16),
            pltpu.VMEM((HD, HD), BF16),
            pltpu.VMEM((2 * JOIN, ROWS), F32),
            pltpu.VMEM((JOIN * TP, 2 * JOIN, ROWS), F32),
            pltpu.VMEM((JOIN, ROWS), F32),
            pltpu.SemaphoreType.DMA((12,)),
            pltpu.SemaphoreType.DMA((12,)),
            pltpu.SemaphoreType.REGULAR((7,)),
        ],
        compiler_params=pltpu.CompilerParams(
            collective_id=0, has_side_effects=True, vmem_limit_bytes=60 << 20
        ),
        name="lightning",
    )(
        position.reshape(1, ROWS), lengths, decay_rates, norm_gain.reshape(1, -1),
        query_rows, key_rows, value_rows, grad_output,
    )
    return pl.pallas_call(
        finish,
        out_shape=(shape,) * 4,
        in_specs=[hbm] * 4,
        out_specs=(hbm,) * 4,
        scratch_shapes=[
            held, held, pltpu.VMEM((JOIN, SLOTS, 2 * HD), BF16), pltpu.VMEM((ROWS, SLOTS), BF16),
            held, held, pltpu.SemaphoreType.DMA((8,)),
        ],
        compiler_params=pltpu.CompilerParams(vmem_limit_bytes=60 << 20),
        name="finish",
    )(*kept)


def solution(mesh):
    rows, specs = P("ctx", "tp"), (P("ctx", "tp"),) * 4
    return jax.shard_map(
        body,
        mesh=mesh,
        in_specs=(rows, rows, rows, P("ctx"), P(), P("tp"), P("tp"), rows),
        out_specs=specs,
        check_vma=False,
    )
```

```python
import jax
import jax.numpy as jnp
from jax import lax
from jax.experimental import pallas as pl
from jax.experimental.pallas import tpu as pltpu
from jax.sharding import PartitionSpec as P

MESH = pl.DeviceIdType.MESH
F32, BF16, I32 = jnp.float32, jnp.bfloat16, jnp.int32
HIGHEST = lax.Precision.HIGHEST
EPSILON = 1e-05
ROWS = 128
HD = 128
JOIN = 4
SPAN = JOIN * ROWS
CTX, TP = 64, 8
GROUPS = CTX // JOIN
CAP = 4 * JOIN
SLOTS = GROUPS * CAP
ARRIVE = CTX * CAP
WIDE = 3 * HD


def dot(a, b, precision=None):
    return jnp.dot(a, b, preferred_element_type=F32, precision=precision)


def dot_nt(a, b, precision=None):
    return lax.dot_general(a, b, (((1,), (1,)), ((), ())), preferred_element_type=F32, precision=precision)


def dot_tn(a, b):
    return lax.dot_general(a, b, (((0,), (0,)), ((), ())), preferred_element_type=F32)


def iota(shape, dim):
    return lax.broadcasted_iota(I32, shape, dim)


def onehot(condition):
    return jnp.where(condition, 1.0, 0.0).astype(BF16)


def column(row):
    return jnp.broadcast_to(row, (ROWS, ROWS)).T


def kernel(
    pos_hbm, len_hbm, rate_hbm, gain_hbm, q_hbm, k_hbm, v_hbm, go_hbm,
    nrm_out, dq_out, got, give_out,
    pos_ref, len_ref, rate_ref, gain_ref, q_ref, k_ref, v_ref, go_ref, lsem,
    snd, rcv, sndq, snd2, pall, u_ref, ut_ref, w_ref, ends, qx, kx, vx, gox, att, attx, dob, pb, dpb,
    nrm_ref, dq_ref, give_ref, rcvq, state, state_in, back, back_in, part, parts, inv_ref, ssem, rsem, known,
):
    c, t = lax.axis_index("ctx"), lax.axis_index("tp")
    grp, k = c // JOIN, lax.rem(c, JOIN)
    own_cols = pl.ds(pl.multiple_of(k * HD, HD), HD)

    loads = [
        pltpu.make_async_copy(src, dst, lsem.at[i])
        for i, (src, dst) in enumerate(
            (
                (pos_hbm, pos_ref), (k_hbm, k_ref), (v_hbm, v_ref), (q_hbm, q_ref),
                (len_hbm, len_ref), (rate_hbm, rate_ref), (gain_hbm, gain_ref), (go_hbm, go_ref),
            )
        )
    ]
    for load in loads:
        load.start()
    own_y, own_z = c // 16, lax.rem(c, 16)

    def step_to(dy, dz):
        return lax.rem(own_y + dy, 4) * 16 + lax.rem(own_z + dz, 16)

    def peer(f):
        turn = f // 4
        h = (turn + 1) // 2
        return step_to(lax.rem(f, 4), jnp.where(lax.rem(turn, 2) == 1, h, 16 - h))

    barrier = pltpu.get_barrier_semaphore()
    near = 12

    @pl.loop(1, near)
    def _(f):
        pl.semaphore_signal(barrier, inc=1, device_id={"ctx": peer(f)}, device_id_type=MESH)

    @pl.loop(1, TP)
    def _(d):
        pl.semaphore_signal(barrier, inc=1, device_id={"tp": lax.rem(t + d, TP)}, device_id_type=MESH)

    def tell(reach, i):
        for j, dz in enumerate((16 - reach, reach)):
            pl.semaphore_signal(known.at[2 * i + j], inc=1, device_id={"ctx": step_to(0, dz)}, device_id_type=MESH)

    def learn(i):
        for j in range(2):
            pl.semaphore_wait(known.at[2 * i + j], 1)

    def remote(src, dst, index, **where):
        return pltpu.make_async_remote_copy(
            src_ref=src, dst_ref=dst, send_sem=ssem.at[index], recv_sem=rsem.at[index],
            device_id=where, device_id_type=MESH,
        )

    def wait(ref, sems, index):
        pltpu.make_async_copy(ref, ref, sems.at[index]).wait()

    loads[0].wait()
    pos = pos_ref[...]
    posr = jnp.broadcast_to(pos, (ROWS, ROWS))
    posc = posr.T
    gr, gc = posr >> 9, posc >> 9
    ri, ci = iota((ROWS, ROWS), 0), iota((ROWS, ROWS), 1)
    same = gr == gc
    rank_row = jnp.sum(jnp.where(same & (ri < ci), 1, 0), axis=0, keepdims=True)
    rank_col = jnp.sum(jnp.where(same & (ci < ri), 1, 0), axis=1, keepdims=True)
    slot_row = gr[:1] * CAP + rank_row
    slot_col = gc[:, :1] * CAP + rank_col
    pick = onehot(iota((SLOTS, ROWS), 0) == slot_row)

    def spread(ref, part_index):
        moved = dot(pick, ref[...]).astype(BF16)
        for h in range(JOIN):
            snd[:, h, :, part_index * HD : (part_index + 1) * HD] = moved[:, h * HD : (h + 1) * HD].reshape(
                GROUPS, CAP, HD
            )

    def send_rows(f, lo, n, index):
        p = peer(f)
        remote(
            snd.at[p // JOIN, lax.rem(p, JOIN), :, pl.ds(lo, n)],
            rcv.at[pl.ds(c * CAP, CAP), pl.ds(lo, n)],
            index, ctx=p,
        ).start()

    def send_stage(first, last):
        @pl.loop((first + 3) // 4, last // 4)
        def _(turn):
            remote(pos_ref, pall.at[pl.ds(c, 1)], 0, ctx=peer(4 * turn)).start()

        @pl.loop(first, last)
        def _(i):
            send_rows(last - 1 + first - i, 0, 2 * HD, 1)

    pl.semaphore_wait(barrier, near - 1 + TP - 1)
    tell(1, 0)
    for i, ref in enumerate((k_ref, v_ref)):
        loads[i + 1].wait()
        spread(ref, i)
    send_stage(1, near)
    learn(0)
    tell(2, 1)
    send_stage(near, 20)
    learn(1)
    tell(4, 2)

    @pl.loop(1, TP)
    def _(d):
        pl.semaphore_signal(known.at[6], inc=1, device_id={"tp": lax.rem(t + d, TP)}, device_id_type=MESH)

    send_stage(20, 36)
    loads[3].wait()
    spread(q_ref, 2)
    learn(2)
    send_stage(36, CTX)

    @pl.loop(1, CTX)
    def _(i):
        send_rows(CTX - i, 2 * HD, HD, 2)

    def mates(fn):
        for d in range(1, JOIN):
            m = lax.rem(k + d, JOIN)
            fn(m, grp * JOIN + m)

    rcv[pl.ds(c * CAP, CAP)] = snd[grp, k]
    pall[pl.ds(c, 1)] = pos
    give_ref[...] = onehot(iota((ROWS, SLOTS), 1) == slot_col)
    stores = [pltpu.make_async_copy(give_ref, give_out, lsem.at[8])]
    stores[0].start()
    for load in loads[4:]:
        load.wait()
    gox[pl.ds(k * ROWS, ROWS)] = go_ref[:, own_cols]

    rate = rate_ref[k]
    start = grp * SPAN
    here = iota((1, SPAN), 1) + start
    doc_row = jnp.full((1, SPAN), -1, I32)
    offset = jnp.int32(0)
    doc_prev, doc_next = jnp.int32(-1), jnp.int32(-1)
    doc_first, doc_last = jnp.int32(-1), jnp.int32(-1)
    for d in range(len_ref.shape[0]):
        doc_row += jnp.where(offset <= here, 1, 0)
        doc_prev += jnp.where(offset <= start - 1, 1, 0)
        doc_first += jnp.where(offset <= start, 1, 0)
        doc_last += jnp.where(offset <= start + SPAN - 1, 1, 0)
        doc_next += jnp.where(offset <= start + SPAN, 1, 0)
        offset += len_ref[d]
    doc_next = jnp.where(grp == GROUPS - 1, -2, doc_next)
    for i in range(JOIN):
        rows = slice(i * ROWS, (i + 1) * ROWS)
        doc_col = column(doc_row[:, rows])
        for j in range(i + 1):
            gap = (ri - ci) + (i - j) * ROWS
            kept = doc_col == doc_row[:, j * ROWS : (j + 1) * ROWS]
            if i == j:
                kept = kept & (gap >= 0)
            decay = jnp.exp(-rate * jnp.maximum(gap, 0).astype(F32))
            w_ref[rows, j * ROWS : (j + 1) * ROWS] = jnp.where(kept, decay, 0.0)
        at = (ri + i * ROWS).astype(F32)
        ends[0, rows] = jnp.where(doc_col == doc_prev, jnp.exp(-rate * (at + 1.0)), 0.0)
        ends[1, rows] = jnp.where(doc_col == doc_next, jnp.exp(-rate * (SPAN - at)), 0.0)
        ends[2, rows] = jnp.where(doc_col == doc_last, jnp.exp(-rate * (SPAN - 1.0 - at)), 0.0)
        ends[3, rows] = jnp.where(doc_col == doc_first, jnp.exp(-rate * at), 0.0)

    wait(pall.at[pl.ds(0, 15)], rsem, 0)
    own_line = pall.at[pl.ds(pl.multiple_of(own_y * 16, 16), 16)]
    for d in range(1, 4):
        remote(own_line, own_line, 9, ctx=lax.rem(own_y + d, 4) * 16 + own_z).start()
    wait(pall.at[pl.ds(0, 48)], rsem, 9)
    everywhere = pall[...]
    ours = everywhere >> 9 == grp
    rank = dot(onehot(ours), onehot(ri < ci))
    place = (everywhere & (SPAN - 1)).astype(F32) + 1.0
    places = jnp.zeros((CTX, ROWS), F32)
    for r in range(CAP):
        held = jnp.sum(jnp.where(ours & (rank == float(r)), place, 0.0), axis=1, keepdims=True)
        places = jnp.where(iota((CTX, ROWS), 1) == r, held, places)
    tile = jnp.where(lax.rem(iota((ROWS, ARRIVE), 1), CAP) == iota((ROWS, ARRIVE), 0), 1.0, 0.0)
    owner = iota((CTX, ARRIVE), 1) // CAP == iota((CTX, ARRIVE), 0)
    place_row = jnp.sum(jnp.where(owner, dot(places, tile, HIGHEST), 0.0), axis=0, keepdims=True) - 1.0
    place_row = place_row.astype(I32)
    for i in range(JOIN):
        rows = slice(i * ROWS, (i + 1) * ROWS)
        u_ref[rows] = onehot(iota((ROWS, ARRIVE), 0) + i * ROWS == place_row)
    for j in range(ARRIVE // ROWS):
        cols = slice(j * ROWS, (j + 1) * ROWS)
        place_col = column(place_row[:, cols])
        for i in range(JOIN):
            ut_ref[cols, i * ROWS : (i + 1) * ROWS] = onehot(place_col == ci + i * ROWS)

    wait(rcv.at[pl.ds(0, ARRIVE - CAP), pl.ds(0, 2 * HD)], rsem, 1)
    kv = dot(u_ref[...], rcv[:, : 2 * HD]).astype(BF16)
    kx[...] = kv[:, :HD]
    vx[...] = kv[:, HD:]
    state[...] = dot_tn((kx[...].astype(F32) * ends[2]).astype(BF16), vx[...]).astype(BF16)
    for i in range(0, HD, 16):
        remote(state.at[pl.ds(i, 16)], state_in.at[pl.ds(i, 16)], 4, ctx=lax.rem(c + JOIN, CTX)).start()
    mates(
        lambda m, p: remote(
            go_ref.at[:, pl.ds(pl.multiple_of(m * HD, HD), HD)], gox.at[pl.ds(k * ROWS, ROWS)], 3, ctx=p
        ).start()
    )

    wait(rcv.at[pl.ds(0, ARRIVE - CAP), pl.ds(2 * HD, HD)], rsem, 2)
    qx[...] = dot(u_ref[...], rcv[:, 2 * HD :]).astype(BF16)
    for i in range(JOIN):
        rows, n = slice(i * ROWS, (i + 1) * ROWS), (i + 1) * ROWS
        pb[rows, :n] = (dot_nt(qx[rows], kx[:n]) * w_ref[rows, :n]).astype(BF16)
    wait(state_in, rsem, 4)
    gain = gain_ref[:, own_cols]
    ones = jnp.ones((8, HD), BF16)

    def row_sums(x):
        high = x.astype(BF16)
        low = (x - high.astype(F32)).astype(BF16)
        return (dot_nt(ones, high) + dot_nt(ones, low))[:1]

    for i in range(JOIN):
        rows, n = slice(i * ROWS, (i + 1) * ROWS), (i + 1) * ROWS
        entered = (qx[rows].astype(F32) * ends[0, rows]).astype(BF16)
        a = (dot(pb[rows, :n], vx[:n]) + dot(entered, state_in[...])).astype(BF16)
        att[rows] = a
        a = a.astype(F32)
        part[i : i + 1] = row_sums(a * a)
    wait(gox.at[pl.ds(0, SPAN - ROWS)], rsem, 3)
    for i in range(JOIN):
        rows = slice(i * ROWS, (i + 1) * ROWS)
        g = gox[rows].astype(F32) * gain
        part[JOIN + i : JOIN + i + 1] = row_sums(g * att[rows].astype(F32))

    pl.semaphore_wait(known.at[6], TP - 1)

    @pl.loop(1, JOIN * TP)
    def _(i):
        m = lax.rem(k + i // TP, JOIN)
        remote(part, parts.at[k * TP + t], 5, ctx=grp * JOIN + m, tp=lax.rem(t + i, TP)).start()

    mates(
        lambda m, p: remote(
            att.at[pl.ds(pl.multiple_of(m * ROWS, ROWS), ROWS)], attx.at[:, own_cols], 7, ctx=p
        ).start()
    )
    attx[:, own_cols] = att[pl.ds(pl.multiple_of(k * ROWS, ROWS), ROWS)]
    parts[k * TP + t] = part[...]
    wait(parts.at[pl.ds(0, JOIN * TP - 1)], rsem, 5)
    total = jnp.sum(parts[...], axis=0)
    width = float(HD * JOIN * TP)
    inverse = lax.rsqrt(total[:JOIN] / width + EPSILON)
    coef = inverse * inverse * inverse * total[JOIN:] / width
    inv_ref[...] = inverse

    carried = jnp.zeros((HD, HD), F32)
    for i in range(JOIN):
        rows = slice(i * ROWS, (i + 1) * ROWS)
        inv, cf = column(inverse[i : i + 1]), column(coef[i : i + 1])
        a = att[rows].astype(F32)
        g = gox[rows].astype(F32) * gain
        d_o = (inv * g - a * cf).astype(BF16)
        dob[rows] = d_o
        carried += dot_tn((qx[rows].astype(F32) * ends[3, rows]).astype(BF16), d_o)
    back[...] = carried.astype(BF16)
    for i in range(0, HD, 16):
        remote(back.at[pl.ds(i, 16)], back_in.at[pl.ds(i, 16)], 8, ctx=lax.rem(c + CTX - JOIN, CTX)).start()

    def send_back(src, dst, index, early):
        def send(p):
            remote(src.at[pl.ds(p * CAP, CAP)], dst.at[k, pl.ds(grp * CAP, CAP)], index, ctx=p).start()

        @pl.loop(0, 4 * early)
        def _(i):
            p = lax.rem(own_y + i, 4) * 16 + i // 4
            pl.when(p != c)(lambda: send(p))

        @pl.loop(1, CTX)
        def _(d):
            p = peer(CTX - d)
            pl.when(lax.rem(p, 16) >= early)(lambda: send(p))

    dq = []
    for i in range(JOIN):
        rows, n = slice(i * ROWS, (i + 1) * ROWS), (i + 1) * ROWS
        dp = (dot_nt(dob[rows], vx[:n]) * w_ref[rows, :n]).astype(BF16)
        dpb[rows, :n] = dp
        entered = (dob[rows].astype(F32) * ends[0, rows]).astype(BF16)
        dq.append((dot(dp, kx[:n]) + dot_nt(entered, state_in[...])).astype(BF16))
    sndq[...] = dot(ut_ref[...], jnp.concatenate(dq, axis=0)).astype(BF16)
    send_back(sndq, rcvq, 10, 6)
    rcvq[k, pl.ds(grp * CAP, CAP)] = sndq[pl.ds(c * CAP, CAP)]

    wait(back_in, rsem, 8)
    dk, dv = [], []
    for j in range(JOIN):
        cols, low = slice(j * ROWS, (j + 1) * ROWS), j * ROWS
        leave = ends[1, cols]
        value = (vx[cols].astype(F32) * leave).astype(BF16)
        key = (kx[cols].astype(F32) * leave).astype(BF16)
        dk.append((dot_tn(dpb[low:, cols], qx[low:]) + dot_nt(value, back_in[...])).astype(BF16))
        dv.append((dot_tn(pb[low:, cols], dob[low:]) + dot(key, back_in[...])).astype(BF16))
    both = jnp.concatenate([jnp.concatenate(dk, axis=0), jnp.concatenate(dv, axis=0)], axis=1)
    snd2[...] = dot(ut_ref[...], both).astype(BF16)
    send_back(snd2, got, 11, 6)
    stores.append(
        pltpu.make_async_copy(snd2.at[pl.ds(c * CAP, CAP)], got.at[k, pl.ds(grp * CAP, CAP)], lsem.at[9])
    )
    stores[-1].start()

    wait(att.at[pl.ds(0, SPAN - ROWS)], rsem, 7)
    inv = column(inv_ref[pl.ds(k, 1)])
    for h in range(JOIN):
        cols = slice(h * HD, (h + 1) * HD)
        nrm_ref[:, cols] = (attx[:, cols].astype(F32) * inv * gain_ref[:, cols]).astype(BF16)
    stores.append(pltpu.make_async_copy(nrm_ref, nrm_out, lsem.at[10]))
    stores[-1].start()

    wait(sndq.at[pl.ds(0, ARRIVE - CAP)], rsem, 10)
    for h in range(JOIN):
        dq_ref[:, h * HD : (h + 1) * HD] = dot(give_ref[...], rcvq[h]).astype(BF16)
    stores.append(pltpu.make_async_copy(dq_ref, dq_out, lsem.at[11]))
    stores[-1].start()
    wait(snd2.at[pl.ds(0, ARRIVE - CAP)], rsem, 11)

    wait(pall.at[pl.ds(0, 15)], ssem, 0)
    wait(rcv.at[pl.ds(0, ARRIVE - CAP), pl.ds(0, 2 * HD)], ssem, 1)
    wait(rcv.at[pl.ds(0, ARRIVE - CAP), pl.ds(2 * HD, HD)], ssem, 2)
    wait(gox.at[pl.ds(0, SPAN - ROWS)], ssem, 3)
    wait(state, ssem, 4)
    wait(parts.at[pl.ds(0, JOIN * TP - 1)], ssem, 5)
    wait(att.at[pl.ds(0, SPAN - ROWS)], ssem, 7)
    wait(back, ssem, 8)
    wait(pall.at[pl.ds(0, 48)], ssem, 9)
    wait(sndq.at[pl.ds(0, ARRIVE - CAP)], ssem, 10)
    wait(snd2.at[pl.ds(0, ARRIVE - CAP)], ssem, 11)
    for store in stores:
        store.wait()


def finish(nrm, dq, got, give, nrm_out, dq_out, dk_out, dv_out, *scratch):
    nrm_ref, dq_ref, got_ref, give_ref, dk_ref, dv_ref, sem = scratch
    halves = [(got.at[:, :, pl.ds(i * HD, HD)], got_ref.at[i]) for i in range(2)]
    loads = [
        pltpu.make_async_copy(src, dst, sem.at[i])
        for i, (src, dst) in enumerate([(give, give_ref)] + halves + [(nrm, nrm_ref), (dq, dq_ref)])
    ]
    stores = [
        pltpu.make_async_copy(src, dst, sem.at[5 + i])
        for i, (src, dst) in enumerate(((dk_ref, dk_out), (dv_ref, dv_out), (nrm_ref, nrm_out), (dq_ref, dq_out)))
    ]
    for load in loads:
        load.start()
    loads[0].wait()

    def moved(i, ref):
        loads[1 + i].wait()
        for h in range(JOIN):
            ref[:, h * HD : (h + 1) * HD] = dot(give_ref[...], got_ref[i, h]).astype(BF16)
        stores[i].start()

    moved(0, dk_ref)
    for load, store in zip(loads[3:], stores[2:]):
        load.wait()
        store.start()
    moved(1, dv_ref)
    for store in stores:
        store.wait()


def body(query_rows, key_rows, value_rows, position, lengths, decay_rates, norm_gain, grad_output):
    hbm = pl.BlockSpec(memory_space=pltpu.HBM)
    shape = jax.ShapeDtypeStruct(query_rows.shape, BF16)
    held = pltpu.VMEM(query_rows.shape, BF16)
    kept = pl.pallas_call(
        kernel,
        out_shape=(
            shape, shape,
            jax.ShapeDtypeStruct((JOIN, SLOTS, 2 * HD), BF16), jax.ShapeDtypeStruct((ROWS, SLOTS), BF16),
        ),
        in_specs=[hbm] * 8,
        out_specs=(hbm,) * 4,
        scratch_shapes=[
            pltpu.VMEM((1, ROWS), I32),
            pltpu.SMEM(lengths.shape, I32),
            pltpu.SMEM(decay_rates.shape, F32),
            pltpu.VMEM((1, JOIN * HD), F32),
            held, held, held, held,
            pltpu.SemaphoreType.DMA((12,)),
            pltpu.VMEM((GROUPS, JOIN, CAP, WIDE), BF16),
            pltpu.VMEM((ARRIVE, WIDE), BF16),
            pltpu.VMEM((ARRIVE, HD), BF16),
            pltpu.VMEM((ARRIVE, 2 * HD), BF16),
            pltpu.VMEM((CTX, ROWS), I32),
            pltpu.VMEM((SPAN, ARRIVE), BF16),
            pltpu.VMEM((ARRIVE, SPAN), BF16),
            pltpu.VMEM((SPAN, SPAN), F32),
            pltpu.VMEM((4, SPAN, HD), F32),
            pltpu.VMEM((SPAN, HD), BF16),
            pltpu.VMEM((SPAN, HD), BF16),
            pltpu.VMEM((SPAN, HD), BF16),
            pltpu.VMEM((SPAN, HD), BF16),
            pltpu.VMEM((SPAN, HD), BF16),
            held,
            pltpu.VMEM((SPAN, HD), BF16),
            pltpu.VMEM((SPAN, SPAN), BF16),
            pltpu.VMEM((SPAN, SPAN), BF16),
            held, held,
            pltpu.VMEM((ROWS, SLOTS), BF16),
            pltpu.VMEM((JOIN, SLOTS, HD), BF16),
            pltpu.VMEM((HD, HD), BF16),
            pltpu.VMEM((HD, HD), BF16),
            pltpu.VMEM((HD, HD), BF16),
            pltpu.VMEM((HD, HD), BF16),
            pltpu.VMEM((2 * JOIN, ROWS), F32),
            pltpu.VMEM((JOIN * TP, 2 * JOIN, ROWS), F32),
            pltpu.VMEM((JOIN, ROWS), F32),
            pltpu.SemaphoreType.DMA((12,)),
            pltpu.SemaphoreType.DMA((12,)),
            pltpu.SemaphoreType.REGULAR((7,)),
        ],
        compiler_params=pltpu.CompilerParams(
            collective_id=0, has_side_effects=True, vmem_limit_bytes=60 << 20
        ),
        name="lightning",
    )(
        position.reshape(1, ROWS), lengths, decay_rates, norm_gain.reshape(1, -1),
        query_rows, key_rows, value_rows, grad_output,
    )
    return pl.pallas_call(
        finish,
        out_shape=(shape,) * 4,
        in_specs=[hbm] * 4,
        out_specs=(hbm,) * 4,
        scratch_shapes=[
            held, held, pltpu.VMEM((2, JOIN, SLOTS, HD), BF16), pltpu.VMEM((ROWS, SLOTS), BF16),
            held, held, pltpu.SemaphoreType.DMA((9,)),
        ],
        compiler_params=pltpu.CompilerParams(vmem_limit_bytes=60 << 20),
        name="finish",
    )(*kept)


def solution(mesh):
    rows, specs = P("ctx", "tp"), (P("ctx", "tp"),) * 4
    return jax.shard_map(
        body,
        mesh=mesh,
        in_specs=(rows, rows, rows, P("ctx"), P(), P("tp"), P("tp"), rows),
        out_specs=specs,
        check_vma=False,
    )
```
